128 devices in a mesh: gx: 8 (over z, y_hi), gy: 8 (over x, core), gz: 2 (over y_lo).
Axes of the slice: x: 4, y: 4 (y_hi: 2, y_lo: 2; y = y_hi * 2 + y_lo), z: 4, core: 2. Of those that a mesh axis runs over, the one named last changes fastest.
Arguments:
- positions: float32 [3, 8, 8, 2, 128], P(None, 'gx', 'gy', 'gz'), may hold values from 0 to 24, as said below
- occupancy: int32 [8, 8, 2, 128], P('gx', 'gy', 'gz'), may hold values from 0 to 1
- neighbours: int32 [56, 8, 8, 2, 128], P(None, 'gx', 'gy', 'gz'), may hold values from 0 to 639, as said below
- keep: int32 [56, 8, 8, 2, 128], P(None, 'gx', 'gy', 'gz'), may hold values from 0 to 1, as said below
- face_x: int32 [8, 8, 2, 2, 64], P('gx', 'gy', 'gz'), may hold values from 0 to 127, as said below
- face_y: int32 [8, 8, 2, 2, 128], P('gx', 'gy', 'gz'), may hold values from 0 to 255, as said below
- face_z: int32 [8, 8, 2, 128], P('gx', 'gy', 'gz'), may hold values from 0 to 511, as said below
- radial_one: float32 [8, 128], replicated, may hold values from -2 to 2
- mix_one: bfloat16 [384, 128], replicated, may hold values from -0.3125 to 0.3125
- embed: float32 [128], replicated, may hold values from -3 to 3
- radial_two: float32 [8, 128], replicated, may hold values from -3 to 3
- mix_two: bfloat16 [384, 128], replicated, may hold values from -0.3125 to 0.3125
- read_one: float32 [128], replicated, may hold values from -0.4375 to 0.4375
- read_hidden: float32 [128, 16], replicated, may hold values from -0.5 to 0.5
- read_out: float32 [16], replicated, may hold values from -1.5 to 1.5
Outputs:
- energies: float32 [8, 8, 2, 128], P('gx', 'gy', 'gz')
- forces: float32 [3, 8, 8, 2, 128], P(None, 'gx', 'gy', 'gz')
The draws below stay inside these ranges and needn't reach their ends.
Inputs may be any that keep to these rules, and one draw needn't show every extreme that they name: `positions`: coordinates in angstrom in the box's own frame; any two atoms named by one list entry lie at least 1.4 apart, counted with the periodic images along gx and gy. `neighbours`: Where the neighbour would lie outside the slab, the entry names the atom at the opposite offset and keep is 0. `keep`: 0 where the atom's slot or the neighbour's slot is empty, or the entry is a pad. `face_x`: distinct own slots; entry 0 lists the slots seen by the lower box, entry 1 by the higher box. `face_y`: distinct rows of the own and x-ghost part of the list; entry 0 for the lower box along gy, entry 1 for the higher. `face_z`: distinct rows of the own, x- and y-ghost part of the list, seen by the other box along gz.
All inputs are finite; a program needn't handle non-finite values.
Results may differ from the reference program's by a relative error of at most 0.01.
Values may be sent and summed in bfloat16 or wider, within the bound.
A program may use at most 128 MiB of HBM per device.

```python
import jax
import jax.numpy as jnp
import numpy as np
from jax import lax

C = 128
NB = 8
HID = 16
NEIGH = 56
DEPTH = 2
LX = 4
LY = 4
LZ = 8
SLOTS = 128
BOXES_X = 8
BOXES_Y = 8
BOXES_Z = 2


SPACING = 1.8


def offsets_table():
    entries = []
    for shift_x in range(-2, 3):
        for shift_y in range(-2, 3):
            for shift_z in range(-2, 3):
                reach_sq = shift_x * shift_x + shift_y * shift_y + shift_z * shift_z
                if 0 < reach_sq <= 5:
                    entries.append((shift_x, shift_y, shift_z))
    return np.array(entries, dtype=np.int32)


def site_coords(site_ids):
    return (site_ids // (LY * LZ), site_ids // LZ % LY, site_ids % LZ)


def slab_plan(key):
    grid_shape = (BOXES_X, BOXES_Y, BOXES_Z)
    scores = jax.random.randint(jax.random.fold_in(key, 11), grid_shape + (SLOTS,), 0, 2 ** 30 // SLOTS)
    scores = scores * SLOTS + jnp.arange(SLOTS, dtype=jnp.int32)
    site_of_slot = jnp.argsort(scores, axis=-1).astype(jnp.int32)
    slot_of_site = jnp.argsort(site_of_slot, axis=-1).astype(jnp.int32)
    vacancy = jax.random.randint(jax.random.fold_in(key, 12), grid_shape + (1,), 0, 31)
    present = (jax.random.randint(jax.random.fold_in(key, 13), grid_shape + (SLOTS,), 0, 100) >= vacancy).astype(jnp.int32)
    return (site_of_slot, slot_of_site, present)


def extended_slot(slot_of_site, coord_x, coord_y, coord_z):
    grid_shape = slot_of_site.shape[:3]
    coord_x, coord_y, coord_z = jnp.broadcast_arrays(jnp.asarray(coord_x).astype(jnp.int32), jnp.asarray(coord_y).astype(jnp.int32), jnp.asarray(coord_z).astype(jnp.int32))
    target_shape = grid_shape + coord_x.shape[-1:]
    coord_x = jnp.broadcast_to(coord_x, target_shape)
    coord_y = jnp.broadcast_to(coord_y, target_shape)
    coord_z = jnp.broadcast_to(coord_z, target_shape)
    x_face_len = DEPTH * LY * LZ
    y_face_len = DEPTH * (LX + 2 * DEPTH) * LZ
    first_end = SLOTS + 2 * x_face_len
    second_end = first_end + 2 * y_face_len
    inside_site = (jnp.clip(coord_x, 0, LX - 1) * LY + jnp.clip(coord_y, 0, LY - 1)) * LZ + jnp.clip(coord_z, 0, LZ - 1)
    result = jnp.take_along_axis(slot_of_site, inside_site, axis=-1)
    x_low = SLOTS + ((coord_x + DEPTH) * LY + coord_y) * LZ + coord_z
    x_high = SLOTS + x_face_len + ((coord_x - LX) * LY + coord_y) * LZ + coord_z
    y_low = first_end + ((coord_x + DEPTH) * DEPTH + coord_y + DEPTH) * LZ + coord_z
    y_high = first_end + y_face_len + ((coord_x + DEPTH) * DEPTH + coord_y - LY) * LZ + coord_z
    z_part = second_end + ((coord_x + DEPTH) * (LY + 2 * DEPTH) + coord_y + DEPTH) * DEPTH + jnp.where(coord_z >= LZ, coord_z - LZ, coord_z + DEPTH)
    result = jnp.where(coord_x < 0, x_low, result)
    result = jnp.where(coord_x >= LX, x_high, result)
    result = jnp.where(coord_y < 0, y_low, result)
    result = jnp.where(coord_y >= LY, y_high, result)
    result = jnp.where((coord_z < 0) | (coord_z >= LZ), z_part, result)
    return result.astype(jnp.int32)


def neighbour_plan(key):
    site_of_slot, slot_of_site, present = slab_plan(key)
    grid_shape = (BOXES_X, BOXES_Y, BOXES_Z)
    full_shape = grid_shape + (NEIGH, SLOTS)
    flat_shape = grid_shape + (NEIGH * SLOTS,)
    offset_table = offsets_table()
    base_x, base_y, base_z = site_coords(np.arange(SLOTS))
    target_x = base_x[None, :] + offset_table[:, 0:1]
    target_y = base_y[None, :] + offset_table[:, 1:2]
    target_z = base_z[None, :] + offset_table[:, 2:3]
    mirror_x = base_x[None, :] - offset_table[:, 0:1]
    mirror_y = base_y[None, :] - offset_table[:, 1:2]
    mirror_z = base_z[None, :] - offset_table[:, 2:3]
    box_x = jnp.arange(BOXES_X).reshape(BOXES_X, 1, 1, 1, 1)
    box_y = jnp.arange(BOXES_Y).reshape(1, BOXES_Y, 1, 1, 1)
    box_z = jnp.arange(BOXES_Z).reshape(1, 1, BOXES_Z, 1, 1)
    outside = (box_z == 0) & (target_z < 0) | (box_z == BOXES_Z - 1) & (target_z >= LZ)
    outside = jnp.broadcast_to(outside, full_shape)
    pick_x = jnp.where(outside, mirror_x, target_x)
    pick_y = jnp.where(outside, mirror_y, target_y)
    pick_z = jnp.where(outside, mirror_z, target_z)
    slots_site = extended_slot(slot_of_site, pick_x.reshape(flat_shape), pick_y.reshape(flat_shape), pick_z.reshape(flat_shape)).reshape(full_shape)
    owner_x = jnp.broadcast_to((box_x + target_x // LX) % BOXES_X, full_shape)
    owner_y = jnp.broadcast_to((box_y + target_y // LY) % BOXES_Y, full_shape)
    owner_z = jnp.broadcast_to((box_z + target_z // LZ) % BOXES_Z, full_shape)
    target_site = jnp.broadcast_to(jnp.asarray((target_x % LX * LY + target_y % LY) * LZ + target_z % LZ), full_shape)
    there_present = present[owner_x, owner_y, owner_z, target_site]
    here_present = jnp.broadcast_to(present[:, :, :, None, :], full_shape)
    keep_site = jnp.where(outside, 0, here_present * there_present)
    slot_order = jnp.broadcast_to(site_of_slot[:, :, :, None, :], full_shape)
    nbr_slot = jnp.take_along_axis(slots_site, slot_order, axis=-1)
    keep_slot = jnp.take_along_axis(keep_site, slot_order, axis=-1)
    return (jnp.moveaxis(nbr_slot, 3, 0).astype(jnp.int32), jnp.moveaxis(keep_slot, 3, 0).astype(jnp.int32))


def draw_positions(key, part):
    site_of_slot, slot_of_site, present = slab_plan(key)
    coord_x, coord_y, coord_z = site_coords(site_of_slot)
    lattice = (jnp.stack([coord_x, coord_y, coord_z]).astype(jnp.float32) + 0.5) * SPACING
    noise_key = jax.random.fold_in(key, 21)
    jitter = jnp.clip(0.1 * jax.random.normal(noise_key, lattice.shape, jnp.float32), -0.2, 0.2)
    return lattice + jitter


def draw_occupancy(key, part):
    site_of_slot, slot_of_site, present = slab_plan(key)
    return jnp.take_along_axis(present, site_of_slot, axis=-1).astype(jnp.int32)


def draw_neighbours(key, part):
    return neighbour_plan(key)[0]


def draw_keep(key, part):
    return neighbour_plan(key)[1]


def draw_face_x(key, part):
    site_of_slot, slot_of_site, present = slab_plan(key)
    x_face_len = DEPTH * LY * LZ
    return jnp.stack([slot_of_site[..., :x_face_len], slot_of_site[..., SLOTS - x_face_len:]], axis=-2).astype(jnp.int32)


def draw_face_y(key, part):
    site_of_slot, slot_of_site, present = slab_plan(key)
    coord_x, lane_y, coord_z = np.meshgrid(np.arange(-DEPTH, LX + DEPTH), np.arange(DEPTH), np.arange(LZ), indexing='ij')
    coord_x = coord_x.reshape(-1)
    lane_y = lane_y.reshape(-1)
    coord_z = coord_z.reshape(-1)
    lower = extended_slot(slot_of_site, coord_x, lane_y, coord_z)
    upper = extended_slot(slot_of_site, coord_x, LY - DEPTH + lane_y, coord_z)
    return jnp.stack([lower, upper], axis=-2).astype(jnp.int32)


def draw_face_z(key, part):
    site_of_slot, slot_of_site, present = slab_plan(key)
    coord_x, coord_y, lane_z = np.meshgrid(np.arange(-DEPTH, LX + DEPTH), np.arange(-DEPTH, LY + DEPTH), np.arange(DEPTH), indexing='ij')
    box_z = jnp.arange(BOXES_Z).reshape(1, 1, BOXES_Z, 1)
    coord_z = jnp.where(box_z == 0, LZ - DEPTH + lane_z.reshape(-1), lane_z.reshape(-1))
    return extended_slot(slot_of_site, coord_x.reshape(-1), coord_y.reshape(-1), coord_z)


def gaussian(own_key, dims, deviation, bound, held_as=jnp.bfloat16):
    values = deviation * jax.random.normal(own_key, dims, jnp.float32)
    return jnp.clip(values, min=-bound, max=bound).astype(held_as)


def setup_inputs(seed: int = 0) -> dict:
    key_of = jax.random.split(jax.random.key(seed), 16)
    return {
        "positions": draw_positions(jax.random.fold_in(key_of[15], 71), 0),
        "occupancy": draw_occupancy(jax.random.fold_in(key_of[15], 71), 0),
        "neighbours": draw_neighbours(jax.random.fold_in(key_of[15], 71), 0),
        "keep": draw_keep(jax.random.fold_in(key_of[15], 71), 0),
        "face_x": draw_face_x(jax.random.fold_in(key_of[15], 71), 0),
        "face_y": draw_face_y(jax.random.fold_in(key_of[15], 71), 0),
        "face_z": draw_face_z(jax.random.fold_in(key_of[15], 71), 0),
        "radial_one": gaussian(key_of[7], (NB, C), NB ** -0.5, 2.0, jnp.float32),
        "mix_one": gaussian(key_of[8], (3 * C, C), (3 * C) ** -0.5, 0.3125),
        "embed": gaussian(key_of[9], (C,), 0.5, 3.0, jnp.float32),
        "radial_two": gaussian(key_of[10], (NB, C), 0.8, 3.0, jnp.float32),
        "mix_two": gaussian(key_of[11], (3 * C, C), (3 * C) ** -0.5, 0.3125),
        "read_one": gaussian(key_of[12], (C,), 0.03, 0.4375, jnp.float32),
        "read_hidden": gaussian(key_of[13], (C, HID), C ** -0.5, 0.5, jnp.float32),
        "read_out": gaussian(key_of[14], (HID,), HID ** -0.5, 1.5, jnp.float32),
    }


SPACING = 1.8
CUTOFF = 5.0
SPREAD = 0.4
HIGHEST = lax.Precision.HIGHEST

def harmonics(unit_vec):
    unit_x, unit_y, unit_z = (unit_vec[0], unit_vec[1], unit_vec[2])
    root_three = 3.0 ** 0.5
    root_fifteen = 15.0 ** 0.5
    root_five = 5.0 ** 0.5
    return jnp.stack([jnp.ones_like(unit_x), root_three * unit_x, root_three * unit_y, root_three * unit_z, root_fifteen * unit_x * unit_y, root_fifteen * unit_y * unit_z, 0.5 * root_five * (3.0 * unit_z * unit_z - 1.0), root_fifteen * unit_x * unit_z, 0.5 * root_fifteen * (unit_x * unit_x - unit_y * unit_y)])

def radial_basis(distance):
    orders = jnp.arange(1, NB + 1).astype(jnp.float32)[:, None, None]
    scaled = distance / CUTOFF
    envelope = jnp.where(scaled < 1.0, (1.0 - scaled * scaled) ** 2, 0.0)
    return (2.0 / CUTOFF) ** 0.5 * jnp.sin(orders * jnp.pi * scaled) / distance * envelope

def edge_frame(source, centre, nbr_slots, edge_weight):
    offset_vec = source[:, nbr_slots] - centre[:, None, :]
    distance = jnp.sqrt(lax.optimization_barrier(jnp.sum(offset_vec * offset_vec, axis=0)))
    return (radial_basis(distance) * edge_weight, harmonics(offset_vec / distance))

def moments_one(source, centre, nbr_slots, edge_weight):
    basis, angular = edge_frame(source, centre, nbr_slots, edge_weight)
    return jnp.einsum('kja,mja->kma', basis, angular, precision=HIGHEST)

def invariants(amplitude):
    return jnp.concatenate([amplitude[:, 0, :], lax.optimization_barrier(jnp.sum(amplitude[:, 1:4, :] ** 2, axis=1)), lax.optimization_barrier(jnp.sum(amplitude[:, 4:9, :] ** 2, axis=1))], axis=1)

def layer_one_tail(moments, radial_one, mix_one, embed):
    amplitude = SPREAD * jnp.einsum('kma,kc->amc', moments, radial_one, precision=HIGHEST)
    mixed_in = invariants(amplitude).astype(jnp.bfloat16)
    return jnp.dot(mixed_in, mix_one, preferred_element_type=jnp.float32) + embed

def pick_block(total_rows):
    block_size = min(total_rows, 1152)
    while total_rows % block_size:
        block_size = block_size - 1
    return block_size

def layer_two(source, features, nbr_slots, edge_weight, occupied, radial_two, mix_two, read_one, read_hidden, read_out):
    edge_count, atom_count = nbr_slots.shape
    block_size = pick_block(atom_count)
    groups = atom_count // block_size
    widened = features.astype(jnp.float32)

    def per_block(pieces):
        block_slots, block_weight, centre, block_occupied, base_rows = pieces
        basis, angular = edge_frame(source, centre, block_slots, block_weight)
        radial = jnp.einsum('kja,kc->jac', basis, radial_two, precision=HIGHEST)
        message = radial * widened[block_slots]
        amplitude = SPREAD * jnp.einsum('mja,jac->amc', angular, message, precision=HIGHEST)
        mixed_rows = jnp.dot(invariants(amplitude).astype(jnp.bfloat16), mix_two, preferred_element_type=jnp.float32) + base_rows
        hidden = jax.nn.silu(jnp.dot(mixed_rows, read_hidden, precision=HIGHEST))
        return block_occupied * (jnp.dot(base_rows, read_one, precision=HIGHEST) + jnp.dot(hidden, read_out, precision=HIGHEST))
    pieces = (nbr_slots.reshape(edge_count, groups, block_size).transpose(1, 0, 2), edge_weight.reshape(edge_count, groups, block_size).transpose(1, 0, 2), source[:, :atom_count].reshape(3, groups, block_size).transpose(1, 0, 2), occupied.reshape(groups, block_size), widened[:atom_count].reshape(groups, block_size, widened.shape[1]))
    return lax.map(per_block, pieces).reshape(atom_count)

def box_take(values, lists, axis_pos):

    def single(values_box, slot_list):
        return jnp.take(values_box, slot_list, axis=axis_pos)
    return jax.vmap(jax.vmap(jax.vmap(single)))(values, lists)

def ghost_positions(coords, face_x, face_y, face_z):
    step_x = jnp.array([LX * SPACING, 0.0, 0.0], jnp.float32)[:, None]
    step_y = jnp.array([0.0, LY * SPACING, 0.0], jnp.float32)[:, None]
    step_z = jnp.array([0.0, 0.0, LZ * SPACING], jnp.float32)[:, None]
    payload = box_take(coords, face_x, 1)
    widened = jnp.concatenate([coords, jnp.roll(payload[..., 1, :], 1, axis=0) - step_x, jnp.roll(payload[..., 0, :], -1, axis=0) + step_x], axis=-1)
    payload = box_take(widened, face_y, 1)
    widened = jnp.concatenate([widened, jnp.roll(payload[..., 1, :], 1, axis=1) - step_y, jnp.roll(payload[..., 0, :], -1, axis=1) + step_y], axis=-1)
    payload = box_take(widened, face_z, 1)
    upward = jnp.where(jnp.arange(BOXES_Z) == 0, 1.0, -1.0).astype(jnp.float32)[None, None, :, None, None]
    return jnp.concatenate([widened, jnp.roll(payload, 1, axis=2) + upward * step_z], axis=-1)

def ghost_features(rows_grid, face_x, face_y, face_z):
    payload = box_take(rows_grid, face_x, 0)
    widened = jnp.concatenate([rows_grid, jnp.roll(payload[:, :, :, 1], 1, axis=0), jnp.roll(payload[:, :, :, 0], -1, axis=0)], axis=3)
    payload = box_take(widened, face_y, 0)
    widened = jnp.concatenate([widened, jnp.roll(payload[:, :, :, 1], 1, axis=1), jnp.roll(payload[:, :, :, 0], -1, axis=1)], axis=3)
    payload = box_take(widened, face_z, 0)
    return jnp.concatenate([widened, jnp.roll(payload, 1, axis=2)], axis=3)

def reference(positions, occupancy, neighbours, keep, face_x, face_y, face_z, radial_one, mix_one, embed, radial_two, mix_two, read_one, read_hidden, read_out):
    grid_shape = occupancy.shape[:3]
    slot_count = occupancy.shape[3]
    box_count = grid_shape[0] * grid_shape[1] * grid_shape[2]
    coords = jnp.moveaxis(positions, 0, 3)
    nbr_slots = jnp.moveaxis(neighbours, 0, 3)
    edge_weight = jnp.moveaxis(keep, 0, 3).astype(jnp.float32)
    occupied = occupancy.astype(jnp.float32)

    def flatten(values):
        return values.reshape((box_count,) + values.shape[3:])

    def first_moments(pieces):
        return moments_one(pieces[0], pieces[0][:, :slot_count], pieces[1], pieces[2])

    def first_tail(moments):
        return layer_one_tail(moments, radial_one, mix_one, embed)

    def second_layer(pieces):
        return layer_two(pieces[0], pieces[1], pieces[2], pieces[3], pieces[4], radial_two, mix_two, read_one, read_hidden, read_out)

    def energy_of(coords_in):
        source = flatten(ghost_positions(coords_in, face_x, face_y, face_z))
        moments = lax.map(jax.checkpoint(first_moments), (source, flatten(nbr_slots), flatten(edge_weight)))
        first_rows = lax.map(first_tail, moments)
        features = ghost_features(first_rows.reshape(grid_shape + first_rows.shape[1:]), face_x, face_y, face_z).astype(jnp.bfloat16)
        energies = lax.map(jax.checkpoint(second_layer), (source, flatten(features), flatten(nbr_slots), flatten(edge_weight), flatten(occupied)))
        return energies.reshape(occupancy.shape)
    energies, pull_back = jax.vjp(energy_of, coords)
    gradient, = pull_back(jnp.ones_like(energies))
    return (energies, -jnp.moveaxis(gradient, 3, 0))
```

```python
import functools
import math

import jax
import jax.numpy as jnp
from jax import lax
from jax.experimental import pallas as pl
from jax.experimental.pallas import tpu as pltpu
from jax.sharding import PartitionSpec as P

F32 = jnp.float32
BF16 = jnp.bfloat16
NB = 8
NM = 9
ATOMS = 128
NEIGH = 56
EXT = 640
C = 128
STEP_XY = 4 * 1.8
STEP_Z = 8 * 1.8
CUTOFF = 5.0
SPREAD = 0.4
HIGHEST = lax.Precision.HIGHEST
R3 = 3.0**0.5
R5 = 5.0**0.5
R15 = 15.0**0.5
MESH = pl.DeviceIdType.MESH

POS, FEAT, GRAD, FORCE = 0, 5, 10, 15
X_UP, X_DOWN, Y_UP, Y_DOWN, Z_SWAP = 0, 1, 2, 3, 4


def nn(a, b, **kw):
    return jnp.dot(a, b, preferred_element_type=F32, **kw)


def nt(a, b, **kw):
    return lax.dot_general(a, b, (((1,), (1,)), ((), ())), preferred_element_type=F32, **kw)


def tn(a, b, **kw):
    return lax.dot_general(a, b, (((0,), (0,)), ((), ())), preferred_element_type=F32, **kw)


def poly(x, coefficients):
    total = coefficients[-1]
    for c in coefficients[-2::-1]:
        total = total * x + c
    return total


COS_C = [(-1.0) ** i * math.pi ** (2 * i) / math.factorial(2 * i) for i in range(8)]
SIN_C = [(-1.0) ** i * math.pi ** (2 * i + 1) / math.factorial(2 * i + 1) for i in range(7)]


def geometry(vx, vy, vz, w, derivative):
    sq = jnp.where(w > 0.0, vx * vx + vy * vy + vz * vz, 1.0)
    inv_r = lax.rsqrt(sq)
    r = sq * inv_r
    ux, uy, uz = vx * inv_r, vy * inv_r, vz * inv_r
    s = jnp.minimum(r * (1.0 / CUTOFF), 1.0)
    t = 1.0 - s * s
    x = s - 0.5
    x2 = x * x
    sin1 = poly(x2, COS_C)
    cos1 = -x * poly(x2, SIN_C)
    p = w * ((2.0 / CUTOFF) ** 0.5 * inv_r)
    pt = p * t
    q = pt * t
    twice = 2.0 * cos1
    sins = [sin1, twice * sin1]
    for k in range(2, NB):
        sins.append(twice * sins[-1] - sins[-2])
    basis = [q * v for v in sins]
    if not derivative:
        return (ux, uy, uz), inv_r, basis, None
    coss = [cos1, twice * cos1 - 1.0]
    for k in range(2, NB):
        coss.append(twice * coss[-1] - coss[-2])
    q5 = q * (math.pi / CUTOFF)
    low = q * inv_r + pt * (s * (4.0 / CUTOFF))
    slopes = [(k + 1.0) * q5 * coss[k] - low * sins[k] for k in range(NB)]
    return (ux, uy, uz), inv_r, basis, slopes


def harmonics(ux, uy, uz):
    return [
        None,
        R3 * ux,
        R3 * uy,
        R3 * uz,
        R15 * ux * uy,
        R15 * uy * uz,
        0.5 * R5 * (3.0 * uz * uz - 1.0),
        R15 * ux * uz,
        0.5 * R15 * (ux * ux - uy * uy),
    ]


def edge_pull(gamma, unit, inv_r, basis, slopes):
    ux, uy, uz = unit
    ang = harmonics(ux, uy, uz)
    q = [gamma(0, k) for k in range(NB)]
    p = [None] * NM
    for m in range(1, NM):
        for k in range(NB):
            value = gamma(m, k)
            q[k] = q[k] + value * ang[m]
            term = value * basis[k]
            p[m] = term if k == 0 else p[m] + term
    radial = q[0] * slopes[0]
    for k in range(1, NB):
        radial = radial + q[k] * slopes[k]
    gx = R3 * p[1] + R15 * (uy * p[4] + uz * p[7] + ux * p[8])
    gy = R3 * p[2] + R15 * (ux * p[4] + uz * p[5] - uy * p[8])
    gz = R3 * p[3] + R15 * (uy * p[5] + ux * p[7]) + (3.0 * R5) * uz * p[6]
    along = radial - (gx * ux + gy * uy + gz * uz) * inv_r
    return gx * inv_r + along * ux, gy * inv_r + along * uy, gz * inv_r + along * uz


def squares(parts):
    total = parts[0] * parts[0]
    for part in parts[1:]:
        total = total + part * part
    return total


def onehot(rows, first, picks):
    ids = lax.broadcasted_iota(jnp.int32, (rows, picks.shape[1]), 0) + first
    return jnp.where(ids == picks, 1.0, 0.0).astype(BF16)


def split3(x):
    hi = x.astype(BF16)
    rest = x - hi.astype(F32)
    mid = rest.astype(BF16)
    low = (rest - mid.astype(F32)).astype(BF16)
    return hi, mid, low


def kernel(
    pos, occ, nbr, keep, fx, fy, fz, r1, mix1, emb, r2, mix2, ro1, rh, ro2,
    e_out, f_out,
    xt, xsend, xcol, key, wgt, weight, ohx, ohy, ohz,
    r1b, r2b, mixt1, mixt2, embb, amp, amp2, inv, ht, hn, hsend, hxrecv, smat, geo, ut,
    gam, dv, dh, gsend, gzr, gyr, gxr, frow, fsend, frecv, dm,
    send, recv,
):
    cx, cy, cz = lax.axis_index("gx"), lax.axis_index("gy"), lax.axis_index("gz")
    nx, ny = lax.axis_size("gx"), lax.axis_size("gy")
    peers = [
        {"gx": lax.rem(cx + 1, nx)},
        {"gx": lax.rem(cx + nx - 1, nx)},
        {"gy": lax.rem(cy + 1, ny)},
        {"gy": lax.rem(cy + ny - 1, ny)},
        {"gz": 1 - cz},
    ]

    def copy(phase, way, src, dst):
        i = phase + way
        return pltpu.make_async_remote_copy(
            src_ref=src, dst_ref=dst, send_sem=send.at[i], recv_sem=recv.at[i],
            device_id=peers[way], device_id_type=MESH,
        )

    barrier = pltpu.get_barrier_semaphore()
    for peer in peers:
        pl.semaphore_signal(barrier, inc=1, device_id=peer, device_id_type=MESH)

    xt[0] = jnp.zeros((8, ATOMS), F32)
    for d in range(3):
        xt[0, d : d + 1, :] = pos[d, 0, 0]
    pick_x = jnp.concatenate([fx[0, 0, 0, 1:2, :], fx[0, 0, 0, 0:1, :]], axis=1)
    pick_up = fy[0, 0, 0, 1:2, :]
    pick_down = fy[0, 0, 0, 0:1, :]
    pick_z = fz[0, 0]

    def lane_pick(picks, blocks):
        wide = jnp.broadcast_to(picks, (8, ATOMS))
        low = wide & (ATOMS - 1)
        total = jnp.take_along_axis(xt[0], low, axis=1)
        for b in range(1, blocks):
            total = jnp.where(wide >= b * ATOMS, jnp.take_along_axis(xt[b], low, axis=1), total)
        return total

    row = lax.broadcasted_iota(jnp.int32, (8, ATOMS), 0)
    lane = lax.broadcasted_iota(jnp.int32, (8, ATOMS), 1)

    xsend[0] = lane_pick(pick_x, 1)
    pl.semaphore_wait(barrier, 5)
    pos_up = copy(POS, X_UP, xsend.at[0], xsend.at[4])
    pos_down = copy(POS, X_DOWN, xsend.at[0], xsend.at[5])
    pos_up.start()
    pos_down.start()

    for j in range(NEIGH):
        kept = keep[j, 0, 0]
        slot = nbr[j, 0, 0]
        key[j : j + 1, :] = jnp.where(kept > 0, slot, -1)
        wgt[j : j + 1, :] = slot
    ohx[...] = onehot(ATOMS, 0, pick_x)
    ohy[:, 0:ATOMS] = onehot(2 * ATOMS, 0, pick_up)
    ohy[:, ATOMS : 2 * ATOMS] = onehot(2 * ATOMS, 0, pick_down)
    ohz[...] = onehot(4 * ATOMS, 0, pick_z)

    def weight_block(i, carry):
        base = i * 64
        rows = [lax.broadcasted_iota(jnp.int32, (8, ATOMS), 0) + base + 8 * t for t in range(8)]
        total = [jnp.zeros((8, ATOMS), F32) for t in range(8)]
        for j in range(NEIGH):
            one = jnp.broadcast_to(key[j : j + 1, :], (8, ATOMS))
            for t in range(8):
                total[t] = total[t] + jnp.where(rows[t] == one, 1.0, 0.0)
        for t in range(8):
            weight[pl.ds(pl.multiple_of(base + 8 * t, 8), 8), :] = total[t]
        return carry

    lax.fori_loop(0, 3, weight_block, 0)
    pos_up.wait()
    pos_down.wait()
    side = jnp.where(row == 0, STEP_XY, 0.0)
    xt[1] = jnp.where(lane < 64, xsend[4] - side, xsend[5] + side)
    xsend[1] = lane_pick(pick_up, 2)
    xsend[2] = lane_pick(pick_down, 2)
    pos_up = copy(POS, Y_UP, xsend.at[1], xsend.at[6])
    pos_down = copy(POS, Y_DOWN, xsend.at[2], xsend.at[7])
    pos_up.start()
    pos_down.start()
    for k in range(NB):
        r1b[k] = SPREAD * jnp.broadcast_to(r1[k : k + 1, :], (C, ATOMS)).T
        r2b[k] = SPREAD * jnp.broadcast_to(r2[k : k + 1, :], (C, ATOMS)).T
    lax.fori_loop(3, 6, weight_block, 0)
    pos_up.wait()
    pos_down.wait()
    side = jnp.where(row == 1, STEP_XY, 0.0)
    xt[2] = xsend[6] - side
    xt[3] = xsend[7] + side
    xsend[3] = lane_pick(pick_z, 4)
    pos_z = copy(POS, Z_SWAP, xsend.at[3], xsend.at[8])
    pos_z.start()
    for b in range(3):
        rows = slice(b * C, (b + 1) * C)
        mixt1[:, rows] = mix1[rows, :].astype(F32).T.astype(BF16)
        mixt2[:, rows] = mix2[rows, :].astype(F32).T.astype(BF16)
    embb[0] = jnp.broadcast_to(emb[...], (C, ATOMS)).T
    embb[1] = jnp.broadcast_to(ro1[...], (C, ATOMS)).T
    lax.fori_loop(6, 10, weight_block, 0)
    for b in range(4):
        xcol[b * ATOMS : (b + 1) * ATOMS, :] = xt[b].T
    pos_z.wait()
    upward = jnp.where(cz == 0, STEP_Z, -STEP_Z)
    xt[4] = xsend[8] + jnp.where(row == 2, upward, 0.0)
    xcol[4 * ATOMS : 5 * ATOMS, :] = xt[4].T

    slots = wgt[...]
    kept = jnp.where(key[...] >= 0, 1.0, 0.0)
    offsets = []
    for d in range(3):
        pieces = []
        for i in range(NEIGH // 8):
            wide = slots[8 * i : 8 * i + 8, :]
            low = wide & (ATOMS - 1)
            got = None
            for b in range(5):
                table = jnp.broadcast_to(xt[b, d : d + 1, :], (8, ATOMS))
                here = jnp.take_along_axis(table, low, axis=1)
                got = here if b == 0 else jnp.where(wide >= b * ATOMS, here, got)
            pieces.append(got - xt[0, d : d + 1, :])
        offsets.append(jnp.concatenate(pieces, axis=0))
    unit, _, basis, _ = geometry(*offsets, kept, False)
    ang = harmonics(*unit)
    for m in range(NM):
        total = None
        for k in range(NB):
            product = basis[k] if m == 0 else basis[k] * ang[m]
            moment = jnp.sum(product, axis=0, keepdims=True)
            term = r1b[k] * moment
            total = term if k == 0 else total + term
        amp[m] = total
    inv[0:C, :] = amp[0].astype(BF16)
    inv[C : 2 * C, :] = squares([amp[m] for m in range(1, 4)]).astype(BF16)
    inv[2 * C :, :] = squares([amp[m] for m in range(4, 9)]).astype(BF16)
    ht[0] = (nn(mixt1[...], inv[...]) + embb[0]).astype(BF16)

    hsend[0] = nn(ht[0], ohx[...]).astype(BF16)
    feat_up = copy(FEAT, X_UP, hsend.at[0], hxrecv.at[0])
    feat_down = copy(FEAT, X_DOWN, hsend.at[0], hxrecv.at[1])
    feat_up.start()
    feat_down.start()

    def planes(i, carry):
        at = pl.ds(pl.multiple_of(i * 16, 16), 16)
        columns = xcol[at, :]
        v = [columns[:, d : d + 1] - xt[0, d : d + 1, :] for d in range(3)]
        unit, inv_r, basis, slopes = geometry(*v, weight[at, :], True)
        for k in range(NB):
            geo[k, at, :] = basis[k]
            geo[NB + k, at, :] = slopes[k]
        for d in range(3):
            geo[2 * NB + d, at, :] = unit[d]
        geo[2 * NB + 3, at, :] = inv_r
        ang = harmonics(*unit)
        for m in range(NM):
            for k in range(NB):
                product = basis[k] if m == 0 else basis[k] * ang[m]
                col = (m * NB + k) * ATOMS
                smat[at, col : col + ATOMS] = product.astype(BF16)
        return carry

    lax.fori_loop(0, 14, planes, 0)
    feat_up.wait()
    feat_down.wait()
    lane_c = lax.broadcasted_iota(jnp.int32, (C, ATOMS), 1)
    ht[1] = jnp.where(lane_c < 64, hxrecv[0].astype(F32), hxrecv[1].astype(F32)).astype(BF16)
    near = jnp.concatenate([ht[0], ht[1]], axis=1)
    picked = nn(near, ohy[...]).astype(BF16)
    hsend[1] = picked[:, :ATOMS]
    hsend[2] = picked[:, ATOMS:]
    feat_up = copy(FEAT, Y_UP, hsend.at[1], ht.at[2])
    feat_down = copy(FEAT, Y_DOWN, hsend.at[2], ht.at[3])
    feat_up.start()
    feat_down.start()
    lax.fori_loop(14, 27, planes, 0)
    feat_up.wait()
    feat_down.wait()
    near = jnp.concatenate([ht[b] for b in range(4)], axis=1)
    hsend[3] = nn(near, ohz[...]).astype(BF16)
    feat_z = copy(FEAT, Z_SWAP, hsend.at[3], ht.at[4])
    feat_z.start()
    lax.fori_loop(27, 40, planes, 0)
    feat_z.wait()

    whole = jnp.concatenate([ht[b] for b in range(5)], axis=1)
    for m in range(NM):
        part = nn(whole, smat[:, m * NB * ATOMS : (m + 1) * NB * ATOMS])
        total = None
        for k in range(NB):
            term = r2b[k] * part[:, k * ATOMS : (k + 1) * ATOMS]
            total = term if k == 0 else total + term
        amp2[m] = total
    inv[0:C, :] = amp2[0].astype(BF16)
    inv[C : 2 * C, :] = squares([amp2[m] for m in range(1, 4)]).astype(BF16)
    inv[2 * C :, :] = squares([amp2[m] for m in range(4, 9)]).astype(BF16)
    own = ht[0].astype(F32)
    h2 = nn(mixt2[...], inv[...]) + own
    pre = tn(rh[...], h2, precision=HIGHEST)
    sig = 1.0 / (1.0 + jnp.exp(-pre))
    filled = occ[0, 0].astype(F32)
    energy = nn(ro1[...], own, precision=HIGHEST) + nn(ro2[...], pre * sig, precision=HIGHEST)
    e_out[0, 0] = filled * energy
    dpre = tn(ro2[...], filled, precision=HIGHEST) * (sig * (1.0 + pre * (1.0 - sig)))
    dh2 = nn(rh[...], dpre, precision=HIGHEST)
    dinv = nn(mix2[...], dh2.astype(BF16))
    for m in range(NM):
        if m == 0:
            g = dinv[0:C]
        elif m < 4:
            g = 2.0 * dinv[C : 2 * C] * amp2[m]
        else:
            g = 2.0 * dinv[2 * C :] * amp2[m]
        for k in range(NB):
            col = (m * NB + k) * ATOMS
            ut[:, col : col + ATOMS] = (r2b[k] * g).astype(BF16)

    dh[4 * ATOMS :, :] = nt(smat[4 * ATOMS :, :], ut[...])
    gsend[4 * ATOMS :, :] = dh[4 * ATOMS :, :].astype(BF16)
    grad_z = copy(GRAD, Z_SWAP, gsend.at[pl.ds(4 * ATOMS, ATOMS), :], gzr)
    grad_z.start()
    dh[0 : 4 * ATOMS, :] = nt(smat[0 : 4 * ATOMS, :], ut[...])
    dh[0:ATOMS, :] += (dh2 + embb[1] * filled).T
    for b in range(5):
        hn[b * ATOMS : (b + 1) * ATOMS, :] = ht[b].astype(F32).T.astype(BF16)
    grad_z.wait()
    dh[0 : 4 * ATOMS, :] += nn(ohz[...], gzr[...])
    gsend[2 * ATOMS : 4 * ATOMS, :] = dh[2 * ATOMS : 4 * ATOMS, :].astype(BF16)
    grad_up = copy(GRAD, Y_UP, gsend.at[pl.ds(3 * ATOMS, ATOMS), :], gyr.at[pl.ds(ATOMS, ATOMS), :])
    grad_down = copy(GRAD, Y_DOWN, gsend.at[pl.ds(2 * ATOMS, ATOMS), :], gyr.at[pl.ds(0, ATOMS), :])
    grad_up.start()
    grad_down.start()

    def load_geo(at):
        return (
            [geo[2 * NB + d, at, :] for d in range(3)],
            geo[2 * NB + 3, at, :],
            [geo[k, at, :] for k in range(NB)],
            [geo[NB + k, at, :] for k in range(NB)],
        )

    def pull_two(b):
        for m in range(NM):
            cols = slice(m * NB * ATOMS, (m + 1) * NB * ATOMS)
            gam[:, cols] = nn(hn[b * ATOMS : (b + 1) * ATOMS, :], ut[:, cols])

        def body(i, carry):
            from_row = pl.ds(pl.multiple_of(i * 8, 8), 8)
            at = pl.ds(pl.multiple_of(b * ATOMS + i * 8, 8), 8)

            def gamma(m, k):
                col = (m * NB + k) * ATOMS
                return gam[from_row, col : col + ATOMS]

            out = edge_pull(gamma, *load_geo(at))
            for d in range(3):
                dv[d, at, :] = out[d]
            return carry

        lax.fori_loop(0, ATOMS // 8, body, 0)

    pull_two(0)
    pull_two(1)
    grad_up.wait()
    grad_down.wait()
    dh[0 : 2 * ATOMS, :] += nn(ohy[...], gyr[...])
    gsend[ATOMS : 2 * ATOMS, :] = dh[ATOMS : 2 * ATOMS, :].astype(BF16)
    half = ATOMS // 2
    grad_up = copy(GRAD, X_UP, gsend.at[pl.ds(ATOMS + half, half), :], gxr.at[pl.ds(half, half), :])
    grad_down = copy(GRAD, X_DOWN, gsend.at[pl.ds(ATOMS, half), :], gxr.at[pl.ds(0, half), :])
    grad_up.start()
    grad_down.start()
    pull_two(2)
    pull_two(3)
    pull_two(4)
    grad_up.wait()
    grad_down.wait()
    dh1 = dh[0:ATOMS, :] + nn(ohx[...], gxr[...])

    dinv = nt(mix1[...], dh1.astype(BF16))
    for m in range(NM):
        if m == 0:
            g = dinv[0:C]
        elif m < 4:
            g = 2.0 * dinv[C : 2 * C] * amp[m]
        else:
            g = 2.0 * dinv[2 * C :] * amp[m]
        moments = SPREAD * nn(r1[...], g, precision=HIGHEST)
        for k in range(NB):
            dm[m * NB + k] = jnp.broadcast_to(moments[k : k + 1, :], (8, ATOMS))

    def pull_one(i, totals):
        at = pl.ds(pl.multiple_of(i * 8, 8), 8)
        out = edge_pull(lambda m, k: dm[m * NB + k], *load_geo(at))
        result = []
        for d in range(3):
            both = out[d] + dv[d, at, :]
            dv[d, at, :] = both
            result.append(totals[d] + both)
        return tuple(result)

    zero = jnp.zeros((8, ATOMS), F32)
    totals = lax.fori_loop(0, EXT // 8, pull_one, (zero, zero, zero))
    ones = jnp.ones((8, ATOMS), F32)
    for d in range(3):
        column = nt(ones, dv[d], precision=HIGHEST)
        frow[d : d + 1, :] = column[0:1, :]
        frow[d : d + 1, 0:ATOMS] = column[0:1, 0:ATOMS] - jnp.sum(totals[d], axis=0, keepdims=True)

    def pack(slot, values):
        fsend[slot] = jnp.zeros((16, ATOMS), BF16)
        for i, part in enumerate(split3(values)):
            fsend[slot, 4 * i : 4 * i + 3, :] = part

    def spread(received, matrix):
        wide = nt(received, matrix)
        return wide[0:3, :] + wide[4:7, :] + wide[8:11, :]

    pack(0, frow[0:3, 4 * ATOMS :])
    force_z = copy(FORCE, Z_SWAP, fsend.at[0], frecv.at[0])
    force_z.start()
    force_z.wait()
    frow[0:3, 0 : 4 * ATOMS] += spread(frecv[0], ohz[...])
    pack(1, frow[0:3, 3 * ATOMS : 4 * ATOMS])
    pack(2, frow[0:3, 2 * ATOMS : 3 * ATOMS])
    force_up = copy(FORCE, Y_UP, fsend.at[1], frecv.at[1])
    force_down = copy(FORCE, Y_DOWN, fsend.at[2], frecv.at[2])
    force_up.start()
    force_down.start()
    force_up.wait()
    force_down.wait()
    frow[0:3, 0 : 2 * ATOMS] += spread(frecv[2], ohy[:, 0:ATOMS]) + spread(frecv[1], ohy[:, ATOMS:])
    pack(3, frow[0:3, ATOMS : 2 * ATOMS])
    force_up = copy(FORCE, X_UP, fsend.at[3], frecv.at[3])
    force_down = copy(FORCE, X_DOWN, fsend.at[3], frecv.at[4])
    force_up.start()
    force_down.start()
    force_up.wait()
    force_down.wait()
    lane_f = lax.broadcasted_iota(jnp.int32, (16, ATOMS), 1)
    merged = jnp.where(lane_f < 64, frecv[4].astype(F32), frecv[3].astype(F32)).astype(BF16)
    total = frow[0:3, 0:ATOMS] + spread(merged, ohx[...])
    for d in range(3):
        f_out[d, 0, 0] = -total[d : d + 1, :]


def per_device(
    positions, occupancy, neighbours, keep, face_x, face_y, face_z, radial_one, mix_one, embed,
    radial_two, mix_two, read_one, read_hidden, read_out,
):
    vmem = pl.BlockSpec(memory_space=pltpu.VMEM)
    cols = NB * NM * ATOMS
    scratch = [
        pltpu.VMEM((5, 8, ATOMS), F32),
        pltpu.VMEM((9, 8, ATOMS), F32),
        pltpu.VMEM((EXT, 8), F32),
        pltpu.VMEM((NEIGH, ATOMS), jnp.int32),
        pltpu.VMEM((NEIGH, ATOMS), jnp.int32),
        pltpu.VMEM((EXT, ATOMS), F32),
        pltpu.VMEM((ATOMS, ATOMS), BF16),
        pltpu.VMEM((2 * ATOMS, 2 * ATOMS), BF16),
        pltpu.VMEM((4 * ATOMS, ATOMS), BF16),
        pltpu.VMEM((NB, C, ATOMS), F32),
        pltpu.VMEM((NB, C, ATOMS), F32),
        pltpu.VMEM((C, 3 * C), BF16),
        pltpu.VMEM((C, 3 * C), BF16),
        pltpu.VMEM((2, C, ATOMS), F32),
        pltpu.VMEM((NM, C, ATOMS), F32),
        pltpu.VMEM((NM, C, ATOMS), F32),
        pltpu.VMEM((3 * C, ATOMS), BF16),
        pltpu.VMEM((5, C, ATOMS), BF16),
        pltpu.VMEM((EXT, C), BF16),
        pltpu.VMEM((4, C, ATOMS), BF16),
        pltpu.VMEM((2, C, ATOMS), BF16),
        pltpu.VMEM((EXT, cols), BF16),
        pltpu.VMEM((2 * NB + 4, EXT, ATOMS), F32),
        pltpu.VMEM((C, cols), BF16),
        pltpu.VMEM((ATOMS, cols), F32),
        pltpu.VMEM((3, EXT, ATOMS), F32),
        pltpu.VMEM((EXT, C), F32),
        pltpu.VMEM((EXT, C), BF16),
        pltpu.VMEM((ATOMS, C), BF16),
        pltpu.VMEM((2 * ATOMS, C), BF16),
        pltpu.VMEM((ATOMS, C), BF16),
        pltpu.VMEM((8, EXT), F32),
        pltpu.VMEM((4, 16, ATOMS), BF16),
        pltpu.VMEM((5, 16, ATOMS), BF16),
        pltpu.VMEM((NB * NM, 8, ATOMS), F32),
        pltpu.SemaphoreType.DMA((20,)),
        pltpu.SemaphoreType.DMA((20,)),
    ]
    return pl.pallas_call(
        kernel,
        out_shape=(
            jax.ShapeDtypeStruct(occupancy.shape, F32),
            jax.ShapeDtypeStruct(positions.shape, F32),
        ),
        in_specs=[vmem] * 15,
        out_specs=(vmem, vmem),
        scratch_shapes=scratch,
        compiler_params=pltpu.CompilerParams(
            collective_id=0, has_side_effects=True, vmem_limit_bytes=56 * 1024 * 1024
        ),
    )(
        positions, occupancy, neighbours, keep, face_x, face_y, face_z, radial_one, mix_one,
        embed.reshape(1, -1), radial_two, mix_two, read_one.reshape(1, -1), read_hidden,
        read_out.reshape(1, -1),
    )


def solution(mesh):
    return jax.shard_map(
        per_device,
        mesh=mesh,
        in_specs=(
            P(None, "gx", "gy", "gz", None),
            P("gx", "gy", "gz", None),
            P(None, "gx", "gy", "gz", None),
            P(None, "gx", "gy", "gz", None),
            P("gx", "gy", "gz", None, None),
            P("gx", "gy", "gz", None, None),
            P("gx", "gy", "gz", None),
            P(),
            P(),
            P(),
            P(),
            P(),
            P(),
            P(),
            P(),
        ),
        out_specs=(P("gx", "gy", "gz", None), P(None, "gx", "gy", "gz", None)),
        check_vma=False,
    )
```

```python
import functools
import math

import jax
import jax.numpy as jnp
from jax import lax
from jax.experimental import pallas as pl
from jax.experimental.pallas import tpu as pltpu
from jax.sharding import PartitionSpec as P

F32 = jnp.float32
BF16 = jnp.bfloat16
NB = 8
NM = 9
ATOMS = 128
NEIGH = 56
EXT = 640
C = 128
STEP_XY = 4 * 1.8
STEP_Z = 8 * 1.8
CUTOFF = 5.0
SPREAD = 0.4
HIGHEST = lax.Precision.HIGHEST
R3 = 3.0**0.5
R5 = 5.0**0.5
R15 = 15.0**0.5
MESH = pl.DeviceIdType.MESH

GROUPS = [(0, 0), (-1, 0), (1, 0), (0, 1), (-1, 1), (1, 1)]
NEAR = [(dx, dy, dz) for dz in (0, 1) for dy in (0, -1, 1) for dx in (-1, 1)]
NEAR += [(0, dy, dz) for dy, dz in GROUPS[:0:-1]]
POS, FEAT, GRAD, FORCE = 0, 1, 2, 3
GROUP = 2 * 128


def nn(a, b, **kw):
    return jnp.dot(a, b, preferred_element_type=F32, **kw)


def nt(a, b, **kw):
    return lax.dot_general(a, b, (((1,), (1,)), ((), ())), preferred_element_type=F32, **kw)


def tn(a, b, **kw):
    return lax.dot_general(a, b, (((0,), (0,)), ((), ())), preferred_element_type=F32, **kw)


def poly(x, coefficients):
    total = coefficients[-1]
    for c in coefficients[-2::-1]:
        total = total * x + c
    return total


COS_C = [(-1.0) ** i * math.pi ** (2 * i) / math.factorial(2 * i) for i in range(8)]
SIN_C = [(-1.0) ** i * math.pi ** (2 * i + 1) / math.factorial(2 * i + 1) for i in range(7)]


def geometry(vx, vy, vz, w, derivative):
    sq = jnp.where(w > 0.0, vx * vx + vy * vy + vz * vz, 1.0)
    inv_r = lax.rsqrt(sq)
    r = sq * inv_r
    ux, uy, uz = vx * inv_r, vy * inv_r, vz * inv_r
    s = jnp.minimum(r * (1.0 / CUTOFF), 1.0)
    t = 1.0 - s * s
    x = s - 0.5
    x2 = x * x
    sin1 = poly(x2, COS_C)
    cos1 = -x * poly(x2, SIN_C)
    p = w * ((2.0 / CUTOFF) ** 0.5 * inv_r)
    pt = p * t
    q = pt * t
    twice = 2.0 * cos1
    sins = [sin1, twice * sin1]
    for k in range(2, NB):
        sins.append(twice * sins[-1] - sins[-2])
    basis = [q * v for v in sins]
    if not derivative:
        return (ux, uy, uz), inv_r, basis, None
    coss = [cos1, twice * cos1 - 1.0]
    for k in range(2, NB):
        coss.append(twice * coss[-1] - coss[-2])
    q5 = q * (math.pi / CUTOFF)
    low = q * inv_r + pt * (s * (4.0 / CUTOFF))
    slopes = [(k + 1.0) * q5 * coss[k] - low * sins[k] for k in range(NB)]
    return (ux, uy, uz), inv_r, basis, slopes


def harmonics(ux, uy, uz):
    return [
        None,
        R3 * ux,
        R3 * uy,
        R3 * uz,
        R15 * ux * uy,
        R15 * uy * uz,
        0.5 * R5 * (3.0 * uz * uz - 1.0),
        R15 * ux * uz,
        0.5 * R15 * (ux * ux - uy * uy),
    ]


def edge_pull(gamma, unit, inv_r, basis, slopes):
    ux, uy, uz = unit
    ang = harmonics(ux, uy, uz)
    q = [gamma(0, k) for k in range(NB)]
    p = [None] * NM
    for m in range(1, NM):
        for k in range(NB):
            value = gamma(m, k)
            q[k] = q[k] + value * ang[m]
            term = value * basis[k]
            p[m] = term if k == 0 else p[m] + term
    radial = q[0] * slopes[0]
    for k in range(1, NB):
        radial = radial + q[k] * slopes[k]
    gx = R3 * p[1] + R15 * (uy * p[4] + uz * p[7] + ux * p[8])
    gy = R3 * p[2] + R15 * (ux * p[4] + uz * p[5] - uy * p[8])
    gz = R3 * p[3] + R15 * (uy * p[5] + ux * p[7]) + (3.0 * R5) * uz * p[6]
    along = radial - (gx * ux + gy * uy + gz * uz) * inv_r
    return gx * inv_r + along * ux, gy * inv_r + along * uy, gz * inv_r + along * uz


def squares(parts):
    total = parts[0] * parts[0]
    for part in parts[1:]:
        total = total + part * part
    return total


def split(x, parts):
    out = []
    for _ in range(parts):
        part = x.astype(BF16)
        out.append(part)
        x = x - part.astype(F32)
    return out


def equal(a, b):
    return jnp.where(a == b, 1.0, 0.0).astype(BF16)


def flip(offset):
    dx, dy, dz = offset
    return (-dx, -dy, dz)


def kernel(
    pos, occ, nbr, keep, fx, fy, fz, r1, mix1, emb, r2, mix2, ro1, rht, ro2,
    e_out, f_out,
    xt, psend, precv, xcol, nbrs, key, weight, hot, ohx, ohxt, oh, oht,
    r1b, r2b, mixt1, mixt2, embb, amp, amp2, inv, ht, hn, hx, hrecv, smat, geo, near, ut,
    gam, dv, dh, gsend, grecv, frow, fsend, frecv, dm, dvl, flat,
    send, recv,
):
    cx, cy, cz = lax.axis_index("gx"), lax.axis_index("gy"), lax.axis_index("gz")
    nx, ny, nz = lax.axis_size("gx"), lax.axis_size("gy"), lax.axis_size("gz")

    def device(offset):
        dx, dy, dz = offset
        return (lax.rem(cx + dx + nx, nx), lax.rem(cy + dy + ny, ny), lax.rem(cz + dz, nz))

    def copy(phase, offset, src, dst):
        i = NEAR.index(offset)
        j = NEAR.index(flip(offset))
        return pltpu.make_async_remote_copy(
            src_ref=src, dst_ref=dst, send_sem=send.at[phase, i], recv_sem=recv.at[phase, j],
            device_id=device(offset), device_id_type=MESH,
        )

    def exchange(phase, source, target):
        copies = [copy(phase, o, source(o), target(o)) for o in NEAR]
        for c in copies:
            c.start()
        return copies

    def finish(copies):
        for c in copies:
            c.wait_recv()
        for c in copies:
            c.wait_send()

    def rows_of(offset, along):
        dx, dy, dz = offset
        base = GROUPS.index((dy, dz)) * GROUP
        if along == 0:
            return pl.ds(base, ATOMS)
        return pl.ds(base + ATOMS + (0 if along < 0 else ATOMS // 2), ATOMS // 2)

    barrier = pltpu.get_barrier_semaphore()
    for offset in NEAR:
        pl.semaphore_signal(barrier, inc=1, device_id=device(offset), device_id_type=MESH)

    row = lax.broadcasted_iota(jnp.int32, (8, ATOMS), 0)
    lane = lax.broadcasted_iota(jnp.int32, (8, ATOMS), 1)

    def pick(ids, tiles):
        low = ids & (ATOMS - 1)
        total = jnp.take_along_axis(tiles[0], low, axis=1)
        for b in range(1, len(tiles)):
            here = jnp.take_along_axis(tiles[b], low, axis=1)
            total = jnp.where(ids >= b * ATOMS, here, total)
        return total

    psend[...] = jnp.zeros((2, 8, ATOMS), F32)
    for d in range(3):
        psend[0, d : d + 1, :] = pos[d, 0, 0]
    psend[0, 3:4, :] = fy[0, 0, 0, 1:2, :].astype(F32)
    psend[0, 4:5, :] = fy[0, 0, 0, 0:1, :].astype(F32)
    psend[0, 5:6, :] = fz[0, 0].astype(F32)
    xt[0] = psend[0]
    pick_x = jnp.concatenate([fx[0, 0, 0, 1:2, :], fx[0, 0, 0, 0:1, :]], axis=1)
    psend[1] = pick(jnp.broadcast_to(pick_x, (8, ATOMS)), [xt[0]])
    pl.semaphore_wait(barrier, len(NEAR))
    copies = exchange(
        POS,
        lambda o: psend.at[1 if o[0] else 0],
        lambda o: precv.at[NEAR.index(flip(o))],
    )

    for j in range(NEIGH):
        kept = keep[j, 0, 0]
        slot = nbr[j, 0, 0]
        key[j : j + 1, :] = jnp.where(kept > 0, slot, -1)
        nbrs[j : j + 1, :] = slot

    def weight_block(i, carry):
        base = pl.multiple_of(i * 32, 32)
        ids = [row + base + 8 * t for t in range(4)]
        total = [jnp.zeros((8, ATOMS), F32) for t in range(4)]
        for j in range(NEIGH):
            one = jnp.broadcast_to(key[j : j + 1, :], (8, ATOMS))
            found = [jnp.where(ids[t] == one, 1.0, 0.0) for t in range(4)]
            hot[pl.ds(base, 32), j * ATOMS : (j + 1) * ATOMS] = jnp.concatenate(found, axis=0).astype(BF16)
            for t in range(4):
                total[t] = total[t] + found[t]
        for t in range(4):
            weight[pl.ds(base + 8 * t, 8), :] = total[t]
        return carry

    lax.fori_loop(0, EXT // 32, weight_block, 0)
    square = (ATOMS, ATOMS)
    sub = lax.broadcasted_iota(jnp.int32, square, 0)
    along = lax.broadcasted_iota(jnp.int32, square, 1)
    ohx[...] = equal(sub, jnp.broadcast_to(pick_x, square))
    ohxt[...] = equal(along.astype(F32), jnp.broadcast_to(pick_x, square).astype(F32).T)
    for k in range(NB):
        r1b[k] = SPREAD * jnp.broadcast_to(r1[k : k + 1, :], (C, ATOMS)).T
        r2b[k] = SPREAD * jnp.broadcast_to(r2[k : k + 1, :], (C, ATOMS)).T
    for b in range(3):
        rows = slice(b * C, (b + 1) * C)
        mixt1[:, rows] = mix1[rows, :].astype(F32).T.astype(BF16)
        mixt2[:, rows] = mix2[rows, :].astype(F32).T.astype(BF16)
    embb[0] = jnp.broadcast_to(emb[...], (C, ATOMS)).T
    embb[1] = jnp.broadcast_to(ro1[...], (C, ATOMS)).T
    finish(copies)

    def received(dx, dy, dz):
        return precv[NEAR.index((dx, dy, dz))]

    def column(dy, dz):
        own = xt[0] if (dy, dz) == (0, 0) else received(0, dy, dz)
        side = jnp.where(lane < ATOMS // 2, received(-1, dy, dz), received(1, dy, dz))
        step = jnp.where(lane < ATOMS // 2, -STEP_XY, STEP_XY)
        side = side + jnp.where(row == 0, step, 0.0)
        shift = jnp.where(row == 1, dy * STEP_XY, 0.0)
        return [own, side] if dy == 0 else [own + shift, side + shift]

    def listed(dy, dz):
        source = received(0, dy, dz)
        at = 3 if dy < 0 else 4
        return jnp.broadcast_to(source[at : at + 1, :], (8, ATOMS)).astype(jnp.int32)

    own, side = column(0, 0)
    xt[1] = side
    low_y, high_y = listed(-1, 0), listed(1, 0)
    xt[2] = pick(low_y, column(-1, 0))
    xt[3] = pick(high_y, column(1, 0))
    other = jnp.broadcast_to(received(0, 0, 1)[5:6, :], (8, ATOMS)).astype(jnp.int32)
    low_bits = other & (ATOMS - 1)
    through_low = jnp.take_along_axis(listed(-1, 1), low_bits, axis=1)
    through_high = jnp.take_along_axis(listed(1, 1), low_bits, axis=1)
    far = jnp.where(other < 2 * ATOMS, other, through_low + 2 * ATOMS)
    far = jnp.where(other < 3 * ATOMS, far, through_high + 4 * ATOMS)
    upward = jnp.where(cz == 0, STEP_Z, -STEP_Z)
    xt[4] = pick(far, column(0, 1) + column(-1, 1) + column(1, 1)) + jnp.where(row == 2, upward, 0.0)

    slots = nbrs[...]
    kept = jnp.where(key[...] >= 0, 1.0, 0.0)
    offsets = []
    for d in range(3):
        tables = [jnp.broadcast_to(xt[b, d : d + 1, :], (8, ATOMS)) for b in range(5)]
        offsets.append(
            jnp.concatenate(
                [pick(slots[8 * i : 8 * i + 8, :], tables) - tables[0] for i in range(NEIGH // 8)],
                axis=0,
            )
        )
    unit, inv_r, basis, slopes = geometry(*offsets, kept, True)
    for k in range(NB):
        near[k] = basis[k]
        near[NB + k] = slopes[k]
    for d in range(3):
        near[2 * NB + d] = unit[d]
    near[2 * NB + 3] = inv_r
    ang = harmonics(*unit)
    for m in range(NM):
        total = None
        for k in range(NB):
            product = basis[k] if m == 0 else basis[k] * ang[m]
            moment = jnp.sum(product, axis=0, keepdims=True)
            term = r1b[k] * moment
            total = term if k == 0 else total + term
        amp[m] = total
    inv[0:C, :] = amp[0].astype(BF16)
    inv[C : 2 * C, :] = squares([amp[m] for m in range(1, 4)]).astype(BF16)
    inv[2 * C :, :] = squares([amp[m] for m in range(4, 9)]).astype(BF16)
    ht[0] = (nn(mixt1[...], inv[...]) + embb[0]).astype(BF16)
    hrecv[0:ATOMS, :] = ht[0].astype(F32).T.astype(BF16)
    hx[...] = nn(ohxt[...], hrecv[0:ATOMS, :]).astype(BF16)
    half = ATOMS // 2

    def feature_source(o):
        if o[0] == 0:
            return hrecv.at[pl.ds(0, ATOMS), :]
        return hx.at[pl.ds(0 if o[0] > 0 else half, half), :]

    copies = exchange(FEAT, feature_source, lambda o: hrecv.at[rows_of(flip(o), -o[0]), :])

    for b in range(5):
        xcol[b * ATOMS : (b + 1) * ATOMS, :] = xt[b].T
    column_ids = [
        jnp.broadcast_to(ids[0:1, :], square).astype(F32).T for ids in (low_y, high_y, far)
    ]
    row_ids = [jnp.broadcast_to(ids[0:1, :], square) for ids in (low_y, high_y, far)]
    at = 0
    for ids, ids_t, blocks in zip(row_ids, column_ids, (2, 2, 6)):
        for b in range(blocks):
            cut = slice(at * ATOMS, (at + 1) * ATOMS)
            oht[cut, :] = equal(sub + b * ATOMS, ids)
            oh[:, cut] = equal((along + b * ATOMS).astype(F32), ids_t)
            at = at + 1

    def planes(i, carry):
        at = pl.ds(pl.multiple_of(i * 16, 16), 16)
        columns = xcol[at, :]
        v = [columns[:, d : d + 1] - xt[0, d : d + 1, :] for d in range(3)]
        unit, inv_r, basis, slopes = geometry(*v, weight[at, :], True)
        for k in range(NB):
            geo[k, at, :] = basis[k]
            geo[NB + k, at, :] = slopes[k]
        for d in range(3):
            geo[2 * NB + d, at, :] = unit[d]
        geo[2 * NB + 3, at, :] = inv_r
        ang = harmonics(*unit)
        for m in range(NM):
            for k in range(NB):
                product = basis[k] if m == 0 else basis[k] * ang[m]
                col = (m * NB + k) * ATOMS
                smat[at, col : col + ATOMS] = product.astype(BF16)
        return carry

    lax.fori_loop(0, EXT // 16, planes, 0)
    finish(copies)
    hn[0:GROUP, :] = hrecv[0:GROUP, :]
    for b, first, blocks in ((2, 0, 2), (3, 2, 2), (4, 4, 6)):
        cut = slice(first * ATOMS, (first + blocks) * ATOMS)
        source = hrecv[GROUP + first * ATOMS : GROUP + (first + blocks) * ATOMS, :]
        hn[b * ATOMS : (b + 1) * ATOMS, :] = nn(oh[:, cut], source).astype(BF16)
    for b in range(1, 5):
        ht[b] = hn[b * ATOMS : (b + 1) * ATOMS, :].astype(F32).T.astype(BF16)

    whole = jnp.concatenate([ht[b] for b in range(5)], axis=1)
    for m in range(NM):
        part = nn(whole, smat[:, m * NB * ATOMS : (m + 1) * NB * ATOMS])
        total = None
        for k in range(NB):
            term = r2b[k] * part[:, k * ATOMS : (k + 1) * ATOMS]
            total = term if k == 0 else total + term
        amp2[m] = total
    inv[0:C, :] = amp2[0].astype(BF16)
    inv[C : 2 * C, :] = squares([amp2[m] for m in range(1, 4)]).astype(BF16)
    inv[2 * C :, :] = squares([amp2[m] for m in range(4, 9)]).astype(BF16)
    own = ht[0].astype(F32)
    h2 = nn(mixt2[...], inv[...]) + own
    pre = nn(rht[...], h2, precision=HIGHEST)
    sig = 1.0 / (1.0 + jnp.exp(-pre))
    filled = occ[0, 0].astype(F32)
    energy = nn(ro1[...], own, precision=HIGHEST) + nn(ro2[...], pre * sig, precision=HIGHEST)
    e_out[0, 0] = filled * energy
    dpre = tn(ro2[...], filled, precision=HIGHEST) * (sig * (1.0 + pre * (1.0 - sig)))
    dh2 = tn(rht[...], dpre, precision=HIGHEST)
    dinv = nn(mix2[...], dh2.astype(BF16))
    for m in range(NM):
        if m == 0:
            g = dinv[0:C]
        elif m < 4:
            g = 2.0 * dinv[C : 2 * C] * amp2[m]
        else:
            g = 2.0 * dinv[2 * C :] * amp2[m]
        for k in range(NB):
            col = (m * NB + k) * ATOMS
            ut[:, col : col + ATOMS] = (r2b[k] * g).astype(BF16)

    ghosts = nt(smat[ATOMS:, :], ut[...]).astype(BF16)
    gsend[ATOMS:GROUP, :] = ghosts[0:ATOMS, :]
    for b, first, blocks in ((1, 0, 2), (2, 2, 2), (3, 4, 6)):
        cut = slice(first * ATOMS, (first + blocks) * ATOMS)
        rows = slice(GROUP + first * ATOMS, GROUP + (first + blocks) * ATOMS)
        gsend[rows, :] = nn(oht[cut, :], ghosts[b * ATOMS : (b + 1) * ATOMS, :]).astype(BF16)
    copies = exchange(
        GRAD,
        lambda o: gsend.at[rows_of(o, o[0]), :],
        lambda o: grecv.at[rows_of(flip(o), o[0]), :],
    )
    dh[...] = nt(smat[0:ATOMS, :], ut[...]) + (dh2 + embb[1] * filled).T

    def load(planes, at):
        return (
            [planes[2 * NB + d, at, :] for d in range(3)],
            planes[2 * NB + 3, at, :],
            [planes[k, at, :] for k in range(NB)],
            [planes[NB + k, at, :] for k in range(NB)],
        )

    zero = jnp.zeros((8, ATOMS), F32)
    totals = (zero, zero, zero)
    for b in range(5):
        for m in range(NM):
            cols = slice(m * NB * ATOMS, (m + 1) * NB * ATOMS)
            gam[:, cols] = nn(hn[b * ATOMS : (b + 1) * ATOMS, :], ut[:, cols])

        def pull_two(i, totals):
            here = pl.ds(pl.multiple_of(i * 8, 8), 8)
            at = pl.ds(pl.multiple_of(b * ATOMS + i * 8, 8), 8)

            def gamma(m, k):
                col = (m * NB + k) * ATOMS
                return gam[here, col : col + ATOMS]

            out = edge_pull(gamma, *load(geo, at))
            for d in range(3):
                dv[d, at, :] = out[d]
            return tuple(totals[d] + out[d] for d in range(3))

        totals = lax.fori_loop(0, ATOMS // 8, pull_two, totals)
    ones = jnp.ones((8, ATOMS), F32)
    for d in range(3):
        line = nt(ones, dv[d], precision=HIGHEST)
        frow[d : d + 1, :] = line[0:1, :]
        frow[d : d + 1, 0:ATOMS] = line[0:1, 0:ATOMS] - jnp.sum(totals[d], axis=0, keepdims=True)
    finish(copies)
    slot_sum = dh[...]
    for g in range(1, 6):
        slot_sum = slot_sum + grecv[g * GROUP : g * GROUP + ATOMS, :].astype(F32)
    pick_sum = grecv[ATOMS:GROUP, :].astype(F32)
    for g in range(1, 6):
        pick_sum = pick_sum + grecv[g * GROUP + ATOMS : (g + 1) * GROUP, :].astype(F32)
    hi, low = split(pick_sum, 2)
    dh1 = slot_sum + nn(ohx[...], hi) + nn(ohx[...], low)

    dinv = nt(mix1[...], dh1.astype(BF16))
    for m in range(NM):
        if m == 0:
            g = dinv[0:C]
        elif m < 4:
            g = 2.0 * dinv[C : 2 * C] * amp[m]
        else:
            g = 2.0 * dinv[2 * C :] * amp[m]
        moments = SPREAD * nn(r1[...], g, precision=HIGHEST)
        for k in range(NB):
            dm[m * NB + k] = jnp.broadcast_to(moments[k : k + 1, :], (8, ATOMS))

    def pull_one(i, carry):
        at = pl.ds(pl.multiple_of(i * 8, 8), 8)
        out = edge_pull(lambda m, k: dm[m * NB + k], *load(near, at))
        for d in range(3):
            for part, value in enumerate(split(out[d], 2)):
                dvl[2 * d + part, at, :] = value.astype(F32)
        return carry

    lax.fori_loop(0, NEIGH // 8, pull_one, 0)
    flat[6:8, :] = jnp.zeros((2, NEIGH * ATOMS), F32)
    for n in range(6):
        for j in range(NEIGH):
            flat[n : n + 1, j * ATOMS : (j + 1) * ATOMS] = dvl[n, j : j + 1, :]
    lines = nt(flat[...].astype(BF16), hot[...])
    for d in range(3):
        frow[d : d + 1, :] += lines[2 * d : 2 * d + 1, :] + lines[2 * d + 1 : 2 * d + 2, :]
        frow[d : d + 1, 0:ATOMS] -= jnp.sum(dvl[2 * d] + dvl[2 * d + 1], axis=0, keepdims=True)

    def thrice(values):
        pad = jnp.zeros((1, values.shape[1]), F32)
        parts = [jnp.concatenate([p.astype(F32), pad], axis=0) for p in split(values, 3)]
        return jnp.concatenate(parts + [jnp.zeros((4, values.shape[1]), F32)], axis=0).astype(BF16)

    def merged(wide):
        return wide[0:3, :] + wide[4:7, :] + wide[8:11, :]

    fsend[...] = jnp.zeros(fsend.shape, F32)
    fsend[0, 0:3, :] = frow[0:3, ATOMS:GROUP]
    at = 0
    for b, blocks in ((2, 2), (3, 2), (4, 6)):
        cut = slice(at * ATOMS, (at + blocks) * ATOMS)
        values = merged(nn(thrice(frow[0:3, b * ATOMS : (b + 1) * ATOMS]), oh[:, cut]))
        for n in range(blocks):
            fsend[1 + at + n, 0:3, :] = values[:, n * ATOMS : (n + 1) * ATOMS]
        at = at + blocks

    def force_source(o):
        g = GROUPS.index((o[1], o[2]))
        return fsend.at[2 * g - 1 + (1 if o[0] else 0)]

    copies = exchange(FORCE, force_source, lambda o: frecv.at[NEAR.index(flip(o))])
    finish(copies)
    slot_sum = frow[0:3, 0:ATOMS]
    from_low = from_high = None
    for dy, dz in GROUPS:
        if (dy, dz) != (0, 0):
            slot_sum = slot_sum + frecv[NEAR.index((0, dy, dz)), 0:3, :]
        up, down = (frecv[NEAR.index((dx, dy, dz)), 0:3, :] for dx in (1, -1))
        from_high = up if from_high is None else from_high + up
        from_low = down if from_low is None else from_low + down
    pick_sum = jnp.where(lane[0:3, :] < half, from_high, from_low)
    total = slot_sum + merged(nt(thrice(pick_sum), ohx[...]))
    for d in range(3):
        f_out[d, 0, 0] = -total[d : d + 1, :]


def per_device(
    positions, occupancy, neighbours, keep, face_x, face_y, face_z, radial_one, mix_one, embed,
    radial_two, mix_two, read_one, read_hidden, read_out,
):
    vmem = pl.BlockSpec(memory_space=pltpu.VMEM)
    cols = NB * NM * ATOMS
    scratch = [
        pltpu.VMEM((5, 8, ATOMS), F32),
        pltpu.VMEM((2, 8, ATOMS), F32),
        pltpu.VMEM((17, 8, ATOMS), F32),
        pltpu.VMEM((EXT, 8), F32),
        pltpu.VMEM((NEIGH, ATOMS), jnp.int32),
        pltpu.VMEM((NEIGH, ATOMS), jnp.int32),
        pltpu.VMEM((EXT, ATOMS), F32),
        pltpu.VMEM((EXT, NEIGH * ATOMS), BF16),
        pltpu.VMEM((ATOMS, ATOMS), BF16),
        pltpu.VMEM((ATOMS, ATOMS), BF16),
        pltpu.VMEM((ATOMS, 10 * ATOMS), BF16),
        pltpu.VMEM((10 * ATOMS, ATOMS), BF16),
        pltpu.VMEM((NB, C, ATOMS), F32),
        pltpu.VMEM((NB, C, ATOMS), F32),
        pltpu.VMEM((C, 3 * C), BF16),
        pltpu.VMEM((C, 3 * C), BF16),
        pltpu.VMEM((2, C, ATOMS), F32),
        pltpu.VMEM((NM, C, ATOMS), F32),
        pltpu.VMEM((NM, C, ATOMS), F32),
        pltpu.VMEM((3 * C, ATOMS), BF16),
        pltpu.VMEM((5, C, ATOMS), BF16),
        pltpu.VMEM((EXT, C), BF16),
        pltpu.VMEM((ATOMS, C), BF16),
        pltpu.VMEM((6 * GROUP, C), BF16),
        pltpu.VMEM((EXT, cols), BF16),
        pltpu.VMEM((2 * NB + 4, EXT, ATOMS), F32),
        pltpu.VMEM((2 * NB + 4, NEIGH, ATOMS), F32),
        pltpu.VMEM((C, cols), BF16),
        pltpu.VMEM((ATOMS, cols), F32),
        pltpu.VMEM((3, EXT, ATOMS), F32),
        pltpu.VMEM((ATOMS, C), F32),
        pltpu.VMEM((6 * GROUP, C), BF16),
        pltpu.VMEM((6 * GROUP, C), BF16),
        pltpu.VMEM((8, EXT), F32),
        pltpu.VMEM((11, 8, ATOMS), F32),
        pltpu.VMEM((17, 8, ATOMS), F32),
        pltpu.VMEM((NB * NM, 8, ATOMS), F32),
        pltpu.VMEM((6, NEIGH, ATOMS), F32),
        pltpu.VMEM((8, NEIGH * ATOMS), F32),
        pltpu.SemaphoreType.DMA((4, 17)),
        pltpu.SemaphoreType.DMA((4, 17)),
    ]
    return pl.pallas_call(
        kernel,
        out_shape=(
            jax.ShapeDtypeStruct(occupancy.shape, F32),
            jax.ShapeDtypeStruct(positions.shape, F32),
        ),
        in_specs=[vmem] * 15,
        out_specs=(vmem, vmem),
        scratch_shapes=scratch,
        compiler_params=pltpu.CompilerParams(
            collective_id=0, has_side_effects=True, vmem_limit_bytes=56 * 1024 * 1024
        ),
    )(
        positions, occupancy, neighbours, keep, face_x, face_y, face_z, radial_one, mix_one,
        embed.reshape(1, -1), radial_two, mix_two, read_one.reshape(1, -1), read_hidden.T,
        read_out.reshape(1, -1),
    )


def solution(mesh):
    return jax.shard_map(
        per_device,
        mesh=mesh,
        in_specs=(
            P(None, "gx", "gy", "gz", None),
            P("gx", "gy", "gz", None),
            P(None, "gx", "gy", "gz", None),
            P(None, "gx", "gy", "gz", None),
            P("gx", "gy", "gz", None, None),
            P("gx", "gy", "gz", None, None),
            P("gx", "gy", "gz", None),
            P(),
            P(),
            P(),
            P(),
            P(),
            P(),
            P(),
            P(),
        ),
        out_specs=(P("gx", "gy", "gz", None), P(None, "gx", "gy", "gz", None)),
        check_vma=False,
    )
```

```python
import functools
import math

import jax
import jax.numpy as jnp
from jax import lax
from jax.experimental import pallas as pl
from jax.experimental.pallas import tpu as pltpu
from jax.sharding import PartitionSpec as P

F32 = jnp.float32
BF16 = jnp.bfloat16
NB = 8
NM = 9
ATOMS = 128
NEIGH = 56
EXT = 640
C = 128
STEP_XY = 4 * 1.8
STEP_Z = 8 * 1.8
CUTOFF = 5.0
SPREAD = 0.4
HIGHEST = lax.Precision.HIGHEST
R3 = 3.0**0.5
R5 = 5.0**0.5
R15 = 15.0**0.5
MESH = pl.DeviceIdType.MESH

GROUPS = [(0, 0), (-1, 0), (1, 0), (0, 1), (-1, 1), (1, 1)]
NEAR = [(dx, dy, dz) for dz in (0, 1) for dy in (0, -1, 1) for dx in (-1, 1)]
NEAR += [(0, dy, dz) for dy, dz in GROUPS[:0:-1]]
POS, FEAT, GRAD, FORCE = 0, 1, 2, 3
GROUP = 2 * 128
TILE = 16
PART = 320


def nn(a, b, **kw):
    return jnp.dot(a, b, preferred_element_type=F32, **kw)


def nt(a, b, **kw):
    return lax.dot_general(a, b, (((1,), (1,)), ((), ())), preferred_element_type=F32, **kw)


def tn(a, b, **kw):
    return lax.dot_general(a, b, (((0,), (0,)), ((), ())), preferred_element_type=F32, **kw)


def poly(x, coefficients):
    total = coefficients[-1]
    for c in coefficients[-2::-1]:
        total = total * x + c
    return total


COS_C = [(-1.0) ** i * math.pi ** (2 * i) / math.factorial(2 * i) for i in range(8)]
SIN_C = [(-1.0) ** i * math.pi ** (2 * i + 1) / math.factorial(2 * i + 1) for i in range(7)]


def geometry(vx, vy, vz, w, derivative):
    sq = jnp.where(w > 0.0, vx * vx + vy * vy + vz * vz, 1.0)
    inv_r = lax.rsqrt(sq)
    r = sq * inv_r
    ux, uy, uz = vx * inv_r, vy * inv_r, vz * inv_r
    s = jnp.minimum(r * (1.0 / CUTOFF), 1.0)
    t = 1.0 - s * s
    x = s - 0.5
    x2 = x * x
    sin1 = poly(x2, COS_C)
    cos1 = -x * poly(x2, SIN_C)
    p = w * ((2.0 / CUTOFF) ** 0.5 * inv_r)
    pt = p * t
    q = pt * t
    twice = 2.0 * cos1
    sins = [sin1, twice * sin1]
    for k in range(2, NB):
        sins.append(twice * sins[-1] - sins[-2])
    basis = [q * v for v in sins]
    if not derivative:
        return (ux, uy, uz), inv_r, basis, None
    coss = [cos1, twice * cos1 - 1.0]
    for k in range(2, NB):
        coss.append(twice * coss[-1] - coss[-2])
    q5 = q * (math.pi / CUTOFF)
    low = q * inv_r + pt * (s * (4.0 / CUTOFF))
    slopes = [(k + 1.0) * q5 * coss[k] - low * sins[k] for k in range(NB)]
    return (ux, uy, uz), inv_r, basis, slopes


def harmonics(ux, uy, uz):
    return [
        None,
        R3 * ux,
        R3 * uy,
        R3 * uz,
        R15 * ux * uy,
        R15 * uy * uz,
        0.5 * R5 * (3.0 * uz * uz - 1.0),
        R15 * ux * uz,
        0.5 * R15 * (ux * ux - uy * uy),
    ]


def edge_pull(gamma, unit, inv_r, basis, slopes):
    ux, uy, uz = unit
    ang = harmonics(ux, uy, uz)
    q = [gamma(0, k) for k in range(NB)]

    def radial_sum(m):
        total = None
        for k in range(NB):
            value = gamma(m, k)
            q[k] = q[k] + value * ang[m]
            term = value * basis[k]
            total = term if total is None else total + term
        return total

    gx, gy, gz = (R3 * radial_sum(m) for m in (1, 2, 3))
    p = R15 * radial_sum(4)
    gx, gy = gx + uy * p, gy + ux * p
    p = R15 * radial_sum(5)
    gy, gz = gy + uz * p, gz + uy * p
    gz = gz + (3.0 * R5) * uz * radial_sum(6)
    p = R15 * radial_sum(7)
    gx, gz = gx + uz * p, gz + ux * p
    p = R15 * radial_sum(8)
    gx, gy = gx + ux * p, gy - uy * p
    radial = q[0] * slopes[0]
    for k in range(1, NB):
        radial = radial + q[k] * slopes[k]
    along = radial - (gx * ux + gy * uy + gz * uz) * inv_r
    return gx * inv_r + along * ux, gy * inv_r + along * uy, gz * inv_r + along * uz


def squares(parts):
    total = parts[0] * parts[0]
    for part in parts[1:]:
        total = total + part * part
    return total


def split(x, parts):
    out = []
    for _ in range(parts):
        part = x.astype(BF16)
        out.append(part)
        x = x - part.astype(F32)
    return out


def equal(a, b):
    return jnp.where(a == b, 1.0, 0.0).astype(BF16)


def over(count, step, body):
    if step == count:
        body(0, step)
        return

    def run(i, carry):
        body(i, step)
        return carry

    lax.fori_loop(0, count // step, run, 0)


def flip(offset):
    dx, dy, dz = offset
    return (-dx, -dy, dz)


def kernel(
    *refs,
):
    given, (e_out, f_out) = refs[:15], refs[15:17]
    held, loaded = refs[17:32], refs[32]
    pos, occ, nbr, keep, fx, fy, fz, r1, mix1, emb, r2, mix2, ro1, rht, ro2 = held
    (
        xt, psend, precv, xcol, nbrs, key, local, weight, hot, ohx, ohxt, oh, oht,
        r1b, r2b, mixt1, mixt2, embb, moments, amp, amp2, pulls, inv, ht, hn, hx, hrecv, smat, geo, near, ut, un, dghost,
        gam, dv, dh, gsend, grecv, frow, fcol, pulled, fsend, frecv, dm, dvl, flat, turned,
        send, recv,
    ) = refs[33:]
    cx, cy, cz = lax.axis_index("gx"), lax.axis_index("gy"), lax.axis_index("gz")
    nx, ny, nz = lax.axis_size("gx"), lax.axis_size("gy"), lax.axis_size("gz")

    def device(offset):
        dx, dy, dz = offset
        return (lax.rem(cx + dx + nx, nx), lax.rem(cy + dy + ny, ny), lax.rem(cz + dz, nz))

    def copy(phase, offset, src, dst):
        i = NEAR.index(offset)
        j = NEAR.index(flip(offset))
        return pltpu.make_async_remote_copy(
            src_ref=src, dst_ref=dst, send_sem=send.at[phase, i], recv_sem=recv.at[phase, j],
            device_id=device(offset), device_id_type=MESH,
        )

    def exchange(phase, source, target):
        copies = [copy(phase, o, source(o), target(o)) for o in NEAR]
        for c in copies:
            c.start()
        return copies

    def finish(copies):
        for c in copies:
            c.wait_recv()
        for c in copies:
            c.wait_send()

    def rows_of(offset, along):
        dx, dy, dz = offset
        base = GROUPS.index((dy, dz)) * GROUP
        if along == 0:
            return pl.ds(base, ATOMS)
        return pl.ds(base + ATOMS + (0 if along < 0 else ATOMS // 2), ATOMS // 2)

    barrier = pltpu.get_barrier_semaphore()
    for offset in NEAR:
        pl.semaphore_signal(barrier, inc=1, device_id=device(offset), device_id_type=MESH)
    loads = [
        pltpu.make_async_copy(given[n], held[n], loaded.at[n]) for n in range(len(held))
    ]
    order = [0, 4, 5, 6, 2, 3, 7, 10, 8, 11, 9, 12, 1, 13, 14]
    for n in order:
        loads[n].start()
    for n in order[:4]:
        loads[n].wait()

    row = lax.broadcasted_iota(jnp.int32, (8, ATOMS), 0)
    lane = lax.broadcasted_iota(jnp.int32, (8, ATOMS), 1)

    def pick(ids, tiles):
        low = ids & (ATOMS - 1)
        total = jnp.take_along_axis(tiles[0], low, axis=1)
        for b in range(1, len(tiles)):
            here = jnp.take_along_axis(tiles[b], low, axis=1)
            total = jnp.where(ids >= b * ATOMS, here, total)
        return total

    psend[...] = jnp.zeros((2, 8, ATOMS), F32)
    for d in range(3):
        psend[0, d : d + 1, :] = pos[d, 0, 0]
    psend[0, 3:4, :] = fy[0, 0, 0, 1:2, :].astype(F32)
    psend[0, 4:5, :] = fy[0, 0, 0, 0:1, :].astype(F32)
    psend[0, 5:6, :] = fz[0, 0].astype(F32)
    xt[0] = psend[0]
    pick_x = jnp.concatenate([fx[0, 0, 0, 1:2, :], fx[0, 0, 0, 0:1, :]], axis=1)
    psend[1] = pick(jnp.broadcast_to(pick_x, (8, ATOMS)), [xt[0]])
    for n in order[4:6]:
        loads[n].wait()
    def list_row(j, carry):
        slot = nbr[j, 0, 0]
        nbrs[pl.ds(j, 1), :] = slot
        value = jnp.where(keep[j, 0, 0] > 0, slot, -1)
        key[pl.ds(j, 1), :] = value
        for b in range(5):
            inside = (value >= b * ATOMS) & (value < (b + 1) * ATOMS)
            inside = jnp.where(inside, value - b * ATOMS, -1).astype(F32)
            local[b, j] = jnp.broadcast_to(inside, (16, ATOMS)).astype(BF16)
        return carry

    lax.fori_loop(0, NEIGH, list_row, 0, unroll=2)
    for n in order[6:]:
        loads[n].wait()
    def spread_row(k, carry):
        r1b[k] = SPREAD * jnp.broadcast_to(r1[pl.ds(k, 1), :], (C, ATOMS)).T
        r2b[k] = SPREAD * jnp.broadcast_to(r2[pl.ds(k, 1), :], (C, ATOMS)).T
        return carry

    lax.fori_loop(0, NB, spread_row, 0)
    for b in range(3):
        rows = slice(b * C, (b + 1) * C)
        mixt1[:, rows] = mix1[rows, :].astype(F32).T.astype(BF16)
        mixt2[:, rows] = mix2[rows, :].astype(F32).T.astype(BF16)
    embb[0] = jnp.broadcast_to(emb[...], (C, ATOMS)).T
    embb[1] = jnp.broadcast_to(ro1[...], (C, ATOMS)).T
    pl.semaphore_wait(barrier, len(NEAR))
    copies = exchange(
        POS,
        lambda o: psend.at[1 if o[0] else 0],
        lambda o: precv.at[NEAR.index(flip(o))],
    )

    row16 = lax.broadcasted_iota(jnp.int32, (16, ATOMS), 0).astype(F32)
    one16 = jnp.ones((16, ATOMS), BF16)
    nil16 = jnp.zeros((16, ATOMS), BF16)

    def weight_block(n, carry):
        b = n // 4
        i = n % 4
        ids = [(row16 + (i * 32 + 16 * t).astype(F32)).astype(BF16) for t in range(2)]
        at = [pl.ds(pl.multiple_of(n * 32 + 16 * t, 16), 16) for t in range(2)]

        def scan(j8, total):
            total = list(total)
            for jj in range(8):
                one = local[b, j8 * 8 + jj]
                to = pl.ds(pl.multiple_of((j8 * 8 + jj) * ATOMS, ATOMS), ATOMS)
                for t in range(2):
                    found = jnp.where(ids[t] == one, one16, nil16)
                    hot[at[t], to] = found
                    total[t] = total[t] + found
            return tuple(total)

        total = lax.fori_loop(0, NEIGH // 8, scan, (nil16, nil16))
        for t in range(2):
            weight[at[t], :] = total[t].astype(F32)
        return carry

    lax.fori_loop(0, EXT // 32, weight_block, 0)
    square = (ATOMS, ATOMS)
    sub = lax.broadcasted_iota(jnp.int32, square, 0)
    along = lax.broadcasted_iota(jnp.int32, square, 1)
    ohx[...] = equal(sub, jnp.broadcast_to(pick_x, square))
    ohxt[...] = equal(along.astype(F32), jnp.broadcast_to(pick_x, square).astype(F32).T)
    finish(copies)

    def received(dx, dy, dz):
        return precv[NEAR.index((dx, dy, dz))]

    def column(dy, dz):
        own = xt[0] if (dy, dz) == (0, 0) else received(0, dy, dz)
        side = jnp.where(lane < ATOMS // 2, received(-1, dy, dz), received(1, dy, dz))
        step = jnp.where(lane < ATOMS // 2, -STEP_XY, STEP_XY)
        side = side + jnp.where(row == 0, step, 0.0)
        shift = jnp.where(row == 1, dy * STEP_XY, 0.0)
        return [own, side] if dy == 0 else [own + shift, side + shift]

    def listed(dy, dz):
        source = received(0, dy, dz)
        at = 3 if dy < 0 else 4
        return jnp.broadcast_to(source[at : at + 1, :], (8, ATOMS)).astype(jnp.int32)

    own, side = column(0, 0)
    xt[1] = side
    low_y, high_y = listed(-1, 0), listed(1, 0)
    xt[2] = pick(low_y, column(-1, 0))
    xt[3] = pick(high_y, column(1, 0))
    other = jnp.broadcast_to(received(0, 0, 1)[5:6, :], (8, ATOMS)).astype(jnp.int32)
    low_bits = other & (ATOMS - 1)
    through_low = jnp.take_along_axis(listed(-1, 1), low_bits, axis=1)
    through_high = jnp.take_along_axis(listed(1, 1), low_bits, axis=1)
    far = jnp.where(other < 2 * ATOMS, other, through_low + 2 * ATOMS)
    far = jnp.where(other < 3 * ATOMS, far, through_high + 4 * ATOMS)
    upward = jnp.where(cz == 0, STEP_Z, -STEP_Z)
    xt[4] = pick(far, column(0, 1) + column(-1, 1) + column(1, 1)) + jnp.where(row == 2, upward, 0.0)

    moments[...] = jnp.zeros(moments.shape, F32)

    def list_tile(i, carry):
        at = pl.ds(pl.multiple_of(i * 8, 8), 8)
        ids = nbrs[at, :]
        kept = jnp.where(key[at, :] >= 0, 1.0, 0.0)
        offset = []
        for d in range(3):
            tables = [jnp.broadcast_to(xt[b, d : d + 1, :], (8, ATOMS)) for b in range(5)]
            offset.append(pick(ids, tables) - tables[0])
        unit, inv_r, basis, slopes = geometry(*offset, kept, True)
        for k in range(NB):
            near[k, at, :] = basis[k]
            near[NB + k, at, :] = slopes[k]
        for d in range(3):
            near[2 * NB + d, at, :] = unit[d]
        near[2 * NB + 3, at, :] = inv_r
        ang = harmonics(*unit)
        for m in range(NM):
            for k in range(NB):
                moments[m * NB + k] += basis[k] if m == 0 else basis[k] * ang[m]
        return carry

    lax.fori_loop(0, NEIGH // 8, list_tile, 0)

    def first_amplitude(m, carry):
        total = None
        for k in range(NB):
            term = r1b[k] * jnp.sum(moments[m * NB + k], axis=0, keepdims=True)
            total = term if k == 0 else total + term
        amp[m] = total
        return carry

    lax.fori_loop(0, NM, first_amplitude, 0)
    inv[0:C, :] = amp[0].astype(BF16)
    inv[C : 2 * C, :] = squares([amp[m] for m in range(1, 4)]).astype(BF16)
    inv[2 * C :, :] = squares([amp[m] for m in range(4, 9)]).astype(BF16)
    ht[0] = (nn(mixt1[...], inv[...]) + embb[0]).astype(BF16)
    hrecv[0:ATOMS, :] = ht[0].T
    hx[...] = nn(ohxt[...], hrecv[0:ATOMS, :]).astype(BF16)
    half = ATOMS // 2

    def feature_source(o):
        if o[0] == 0:
            return hrecv.at[pl.ds(0, ATOMS), :]
        return hx.at[pl.ds(0 if o[0] > 0 else half, half), :]

    copies = exchange(FEAT, feature_source, lambda o: hrecv.at[rows_of(flip(o), -o[0]), :])

    for b in range(5):
        xcol[b * ATOMS : (b + 1) * ATOMS, :] = xt[b].T
    column_ids = [
        jnp.broadcast_to(ids[0:1, :], square).astype(F32).T for ids in (low_y, high_y, far)
    ]
    row_ids = [jnp.broadcast_to(ids[0:1, :], square) for ids in (low_y, high_y, far)]
    at = 0
    for ids, ids_t, blocks in zip(row_ids, column_ids, (2, 2, 6)):
        for b in range(blocks):
            cut = slice(at * ATOMS, (at + 1) * ATOMS)
            oht[cut, :] = equal(sub + b * ATOMS, ids)
            oh[:, cut] = equal((along + b * ATOMS).astype(F32), ids_t)
            at = at + 1

    def planes(i, carry):
        at = pl.ds(pl.multiple_of(i * 16, 16), 16)
        columns = xcol[at, :]
        v = [columns[:, d : d + 1] - xt[0, d : d + 1, :] for d in range(3)]
        unit, inv_r, basis, slopes = geometry(*v, weight[at, :], True)
        for k in range(NB):
            geo[k, at, :] = basis[k]
            geo[NB + k, at, :] = slopes[k]
        for d in range(3):
            geo[2 * NB + d, at, :] = unit[d]
        geo[2 * NB + 3, at, :] = inv_r
        ang = harmonics(*unit)
        for m in range(NM):
            for k in range(NB):
                product = basis[k] if m == 0 else basis[k] * ang[m]
                col = (m * NB + k) * ATOMS
                smat[at, col : col + ATOMS] = product.astype(BF16)
        return carry

    lax.fori_loop(0, EXT // 16, planes, 0)
    def chunk(m, step=1):
        width = NB * ATOMS * step
        if isinstance(m, int):
            return pl.ds(m * width, width)
        return pl.ds(pl.multiple_of(m * width, width), width)

    def amplitude(m, source, rows):
        part = nn(source, smat[rows, chunk(m)])
        total = None
        for k in range(NB):
            term = r2b[k] * part[:, k * ATOMS : (k + 1) * ATOMS]
            total = term if k == 0 else total + term
        return total

    def amplitude_own(i, step):
        for t in range(step):
            amp2[i * step + t] = amplitude(i * step + t, ht[0], slice(0, ATOMS))

    over(NM, 3, amplitude_own)
    finish(copies)
    hn[0:GROUP, :] = hrecv[0:GROUP, :]
    for b, first, blocks in ((2, 0, 2), (3, 2, 2), (4, 4, 6)):
        cut = slice(first * ATOMS, (first + blocks) * ATOMS)
        source = hrecv[GROUP + first * ATOMS : GROUP + (first + blocks) * ATOMS, :]
        hn[b * ATOMS : (b + 1) * ATOMS, :] = nn(oh[:, cut], source).astype(BF16)
    for b in range(1, 5):
        ht[b] = hn[b * ATOMS : (b + 1) * ATOMS, :].T

    whole = jnp.concatenate([ht[b] for b in range(1, 5)], axis=1)
    def amplitude_ghosts(i, step):
        for t in range(step):
            amp2[i * step + t] += amplitude(i * step + t, whole, slice(ATOMS, EXT))

    over(NM, 9, amplitude_ghosts)
    inv[0:C, :] = amp2[0].astype(BF16)
    inv[C : 2 * C, :] = squares([amp2[m] for m in range(1, 4)]).astype(BF16)
    inv[2 * C :, :] = squares([amp2[m] for m in range(4, 9)]).astype(BF16)
    own = ht[0].astype(F32)
    h2 = nn(mixt2[...], inv[...]) + own
    pre = nn(rht[...], h2, precision=HIGHEST)
    sig = 1.0 / (1.0 + jnp.exp(-pre))
    filled = occ[0, 0].astype(F32)
    energy = nn(ro1[...], own, precision=HIGHEST) + nn(ro2[...], pre * sig, precision=HIGHEST)
    e_out[0, 0] = filled * energy
    dpre = tn(ro2[...], filled, precision=HIGHEST) * (sig * (1.0 + pre * (1.0 - sig)))
    dh2 = tn(rht[...], dpre, precision=HIGHEST)
    dinv = nn(mix2[...], dh2.astype(BF16))
    pulls[...] = dinv

    def pulled_amplitude(m, values):
        square = jnp.where(m < 4, pulls[C : 2 * C, :], pulls[2 * C :, :])
        return jnp.where(m == 0, pulls[0:C, :], 2.0 * square * values[m])

    def rows_two(m, carry):
        g = pulled_amplitude(m, amp2)
        turned = SPREAD * g.T
        for k in range(NB):
            at = pl.ds(pl.multiple_of((m * NB + k) * ATOMS, ATOMS), ATOMS)
            ut[:, at] = (r2b[k] * g).astype(BF16)
            un[at, :] = (turned * r2[k : k + 1, :]).astype(BF16)
        return carry

    lax.fori_loop(0, NM, rows_two, 0)

    def ghost_part(i, step):
        part = nn(smat[ATOMS:, chunk(i, step)], un[chunk(i, step), :])
        if step == NM:
            dghost[...] = part
        else:
            dghost[...] += part

    if 9 < NM:
        dghost[...] = jnp.zeros(dghost.shape, F32)
    over(NM, 9, ghost_part)
    ghosts = dghost[...].astype(BF16)
    gsend[ATOMS:GROUP, :] = ghosts[0:ATOMS, :]
    for b, first, blocks in ((1, 0, 2), (2, 2, 2), (3, 4, 6)):
        cut = slice(first * ATOMS, (first + blocks) * ATOMS)
        rows = slice(GROUP + first * ATOMS, GROUP + (first + blocks) * ATOMS)
        gsend[rows, :] = nn(oht[cut, :], ghosts[b * ATOMS : (b + 1) * ATOMS, :]).astype(BF16)
    copies = exchange(
        GRAD,
        lambda o: gsend.at[rows_of(o, o[0]), :],
        lambda o: grecv.at[rows_of(flip(o), o[0]), :],
    )
    dh[...] = (dh2 + embb[1] * filled).T

    def own_part(i, step):
        dh[...] += nn(smat[0:ATOMS, chunk(i, step)], un[chunk(i, step), :])

    over(NM, 3, own_part)

    def load(planes, at):
        return (
            [planes[2 * NB + d, at, :] for d in range(3)],
            planes[2 * NB + 3, at, :],
            [planes[k, at, :] for k in range(NB)],
            [planes[NB + k, at, :] for k in range(NB)],
        )

    zero = jnp.zeros((TILE, ATOMS), F32)
    totals = (zero, zero, zero)

    def pull_part(b, totals):
        base = pl.multiple_of(b * PART, PART)

        def gammas(i, step):
            for t in range(step):
                at = chunk(i * step + t)
                gam[:, at] = nn(hn[pl.ds(base, PART), :], ut[:, at])

        over(NM, 9, gammas)

        def pull_two(i, totals):
            here = pl.ds(pl.multiple_of(i * TILE, TILE), TILE)
            at = pl.ds(pl.multiple_of(base + i * TILE, TILE), TILE)

            def gamma(m, k):
                col = (m * NB + k) * ATOMS
                return gam[here, col : col + ATOMS]

            out = edge_pull(gamma, *load(geo, at))
            for d in range(3):
                dv[d, at, :] = out[d]
            return tuple(totals[d] + out[d] for d in range(3))

        return lax.fori_loop(0, PART // TILE, pull_two, totals)

    totals = lax.fori_loop(0, EXT // PART, pull_part, totals)
    total = None
    for d in range(3):
        take = jnp.where(along == 2 * d, 1.0, 0.0).astype(BF16)
        for part in split(dv[d], 2):
            term = nn(part, take)
            total = term if total is None else total + term
    fcol[...] = total
    for d in range(3):
        pulled[d : d + 1, :] = jnp.sum(totals[d], axis=0, keepdims=True)
    finish(copies)
    slot_sum = dh[...]
    for g in range(1, 6):
        slot_sum = slot_sum + grecv[g * GROUP : g * GROUP + ATOMS, :].astype(F32)
    pick_sum = grecv[ATOMS:GROUP, :].astype(F32)
    for g in range(1, 6):
        pick_sum = pick_sum + grecv[g * GROUP + ATOMS : (g + 1) * GROUP, :].astype(F32)
    hi, low = split(pick_sum, 2)
    dh1 = slot_sum + nn(ohx[...], hi) + nn(ohx[...], low)

    dinv = nt(mix1[...], dh1.astype(BF16))
    pulls[...] = dinv

    def rows_one(m, carry):
        lines = SPREAD * nn(r1[...], pulled_amplitude(m, amp), precision=HIGHEST)
        for k in range(NB):
            dm[m * NB + k] = jnp.broadcast_to(lines[k : k + 1, :], (8, ATOMS))
        return carry

    lax.fori_loop(0, NM, rows_one, 0)

    def pull_one(i, carry):
        at = pl.ds(pl.multiple_of(i * 8, 8), 8)
        out = edge_pull(lambda m, k: dm[m * NB + k], *load(near, at))
        for d in range(3):
            for part, value in enumerate(split(out[d], 2)):
                dvl[2 * d + part, at, :] = value.astype(F32)
        return carry

    lax.fori_loop(0, NEIGH // 8, pull_one, 0)
    flat[6:8, :] = jnp.zeros((2, NEIGH * ATOMS), F32)

    def flat_row(j, carry):
        to = pl.ds(pl.multiple_of(j * ATOMS, ATOMS), ATOMS)
        for n in range(6):
            flat[n : n + 1, to] = dvl[n, pl.ds(j, 1), :]
        return carry

    lax.fori_loop(0, NEIGH, flat_row, 0, unroll=4)

    def turn(n, carry):
        at = pl.ds(pl.multiple_of(n * 8 * ATOMS, 8 * ATOMS), 8 * ATOMS)
        turned[at, :] = flat[:, at].T.astype(BF16)
        return carry

    lax.fori_loop(0, NEIGH // 8, turn, 0)

    def lines_of(first, last):
        def part(i, step):
            at = chunk(i, step)
            fcol[first:last, 0:8] += nn(hot[first:last, at], turned[at, :])

        over(NEIGH // 8, 7, part)
        for b in range(first // ATOMS, last // ATOMS):
            lines = fcol[b * ATOMS : (b + 1) * ATOMS, 0:8].T
            for d in range(3):
                line = lines[2 * d : 2 * d + 1, :] + lines[2 * d + 1 : 2 * d + 2, :]
                frow[d : d + 1, b * ATOMS : (b + 1) * ATOMS] = line

    lines_of(ATOMS, EXT)

    def thrice(values):
        pad = jnp.zeros((1, values.shape[1]), F32)
        parts = [jnp.concatenate([p.astype(F32), pad], axis=0) for p in split(values, 3)]
        return jnp.concatenate(parts + [jnp.zeros((4, values.shape[1]), F32)], axis=0).astype(BF16)

    def merged(wide):
        return wide[0:3, :] + wide[4:7, :] + wide[8:11, :]

    fsend[...] = jnp.zeros(fsend.shape, F32)
    fsend[0, 0:3, :] = frow[0:3, ATOMS:GROUP]
    at = 0
    for b, blocks in ((2, 2), (3, 2), (4, 6)):
        cut = slice(at * ATOMS, (at + blocks) * ATOMS)
        values = merged(nn(thrice(frow[0:3, b * ATOMS : (b + 1) * ATOMS]), oh[:, cut]))
        for n in range(blocks):
            fsend[1 + at + n, 0:3, :] = values[:, n * ATOMS : (n + 1) * ATOMS]
        at = at + blocks

    def force_source(o):
        g = GROUPS.index((o[1], o[2]))
        return fsend.at[2 * g - 1 + (1 if o[0] else 0)]

    copies = exchange(FORCE, force_source, lambda o: frecv.at[NEAR.index(flip(o))])
    lines_of(0, ATOMS)
    for d in range(3):
        pulled[d : d + 1, :] += jnp.sum(dvl[2 * d] + dvl[2 * d + 1], axis=0, keepdims=True)
    finish(copies)
    slot_sum = frow[0:3, 0:ATOMS] - pulled[0:3, :]
    from_low = from_high = None
    for dy, dz in GROUPS:
        if (dy, dz) != (0, 0):
            slot_sum = slot_sum + frecv[NEAR.index((0, dy, dz)), 0:3, :]
        up, down = (frecv[NEAR.index((dx, dy, dz)), 0:3, :] for dx in (1, -1))
        from_high = up if from_high is None else from_high + up
        from_low = down if from_low is None else from_low + down
    pick_sum = jnp.where(lane[0:3, :] < half, from_high, from_low)
    total = slot_sum + merged(nt(thrice(pick_sum), ohx[...]))
    for d in range(3):
        f_out[d, 0, 0] = -total[d : d + 1, :]


def per_device(
    positions, occupancy, neighbours, keep, face_x, face_y, face_z, radial_one, mix_one, embed,
    radial_two, mix_two, read_one, read_hidden, read_out,
):
    vmem = pl.BlockSpec(memory_space=pltpu.VMEM)
    cols = NB * NM * ATOMS
    operands = (
        positions, occupancy, neighbours, keep, face_x, face_y, face_z, radial_one, mix_one,
        embed.reshape(1, -1), radial_two, mix_two, read_one.reshape(1, -1), read_hidden.T,
        read_out.reshape(1, -1),
    )
    scratch = [pltpu.VMEM(v.shape, v.dtype) for v in operands]
    scratch += [
        pltpu.SemaphoreType.DMA((len(operands),)),
        pltpu.VMEM((5, 8, ATOMS), F32),
        pltpu.VMEM((2, 8, ATOMS), F32),
        pltpu.VMEM((17, 8, ATOMS), F32),
        pltpu.VMEM((EXT, 8), F32),
        pltpu.VMEM((NEIGH, ATOMS), jnp.int32),
        pltpu.VMEM((NEIGH, ATOMS), jnp.int32),
        pltpu.VMEM((5, NEIGH, 16, ATOMS), BF16),
        pltpu.VMEM((EXT, ATOMS), F32),
        pltpu.VMEM((EXT, NEIGH * ATOMS), BF16),
        pltpu.VMEM((ATOMS, ATOMS), BF16),
        pltpu.VMEM((ATOMS, ATOMS), BF16),
        pltpu.VMEM((ATOMS, 10 * ATOMS), BF16),
        pltpu.VMEM((10 * ATOMS, ATOMS), BF16),
        pltpu.VMEM((NB, C, ATOMS), F32),
        pltpu.VMEM((NB, C, ATOMS), F32),
        pltpu.VMEM((C, 3 * C), BF16),
        pltpu.VMEM((C, 3 * C), BF16),
        pltpu.VMEM((2, C, ATOMS), F32),
        pltpu.VMEM((NB * NM, 8, ATOMS), F32),
        pltpu.VMEM((NM, C, ATOMS), F32),
        pltpu.VMEM((NM, C, ATOMS), F32),
        pltpu.VMEM((3 * C, ATOMS), F32),
        pltpu.VMEM((3 * C, ATOMS), BF16),
        pltpu.VMEM((5, C, ATOMS), BF16),
        pltpu.VMEM((EXT, C), BF16),
        pltpu.VMEM((ATOMS, C), BF16),
        pltpu.VMEM((6 * GROUP, C), BF16),
        pltpu.VMEM((EXT, cols), BF16),
        pltpu.VMEM((2 * NB + 4, EXT, ATOMS), F32),
        pltpu.VMEM((2 * NB + 4, NEIGH, ATOMS), F32),
        pltpu.VMEM((C, cols), BF16),
        pltpu.VMEM((cols, C), BF16),
        pltpu.VMEM((4 * ATOMS, C), F32),
        pltpu.VMEM((PART, cols), F32),
        pltpu.VMEM((3, EXT, ATOMS), F32),
        pltpu.VMEM((ATOMS, C), F32),
        pltpu.VMEM((6 * GROUP, C), BF16),
        pltpu.VMEM((6 * GROUP, C), BF16),
        pltpu.VMEM((8, EXT), F32),
        pltpu.VMEM((EXT, ATOMS), F32),
        pltpu.VMEM((8, ATOMS), F32),
        pltpu.VMEM((11, 8, ATOMS), F32),
        pltpu.VMEM((17, 8, ATOMS), F32),
        pltpu.VMEM((NB * NM, 8, ATOMS), F32),
        pltpu.VMEM((6, NEIGH, ATOMS), F32),
        pltpu.VMEM((8, NEIGH * ATOMS), F32),
        pltpu.VMEM((NEIGH * ATOMS, 8), BF16),
        pltpu.SemaphoreType.DMA((4, 17)),
        pltpu.SemaphoreType.DMA((4, 17)),
    ]
    return pl.pallas_call(
        kernel,
        out_shape=(
            jax.ShapeDtypeStruct(occupancy.shape, F32),
            jax.ShapeDtypeStruct(positions.shape, F32),
        ),
        in_specs=[pl.BlockSpec(memory_space=pl.ANY)] * len(operands),
        out_specs=(vmem, vmem),
        scratch_shapes=scratch,
        compiler_params=pltpu.CompilerParams(
            collective_id=0, has_side_effects=True, vmem_limit_bytes=56 * 1024 * 1024
        ),
    )(*operands)


def solution(mesh):
    return jax.shard_map(
        per_device,
        mesh=mesh,
        in_specs=(
            P(None, "gx", "gy", "gz", None),
            P("gx", "gy", "gz", None),
            P(None, "gx", "gy", "gz", None),
            P(None, "gx", "gy", "gz", None),
            P("gx", "gy", "gz", None, None),
            P("gx", "gy", "gz", None, None),
            P("gx", "gy", "gz", None),
            P(),
            P(),
            P(),
            P(),
            P(),
            P(),
            P(),
            P(),
        ),
        out_specs=(P("gx", "gy", "gz", None), P(None, "gx", "gy", "gz", None)),
        check_vma=False,
    )
```

```python
import functools
import math

import jax
import jax.numpy as jnp
from jax import lax
from jax.experimental import pallas as pl
from jax.experimental.pallas import tpu as pltpu
from jax.sharding import PartitionSpec as P

F32 = jnp.float32
BF16 = jnp.bfloat16
NB = 8
NM = 9
ATOMS = 128
NEIGH = 56
EXT = 640
C = 128
STEP_XY = 4 * 1.8
STEP_Z = 8 * 1.8
CUTOFF = 5.0
SPREAD = 0.4
HIGHEST = lax.Precision.HIGHEST
R3 = 3.0**0.5
R5 = 5.0**0.5
R15 = 15.0**0.5
MESH = pl.DeviceIdType.MESH

GROUPS = [(0, 0), (-1, 0), (1, 0), (0, 1), (-1, 1), (1, 1)]
NEAR = [(dx, dy, dz) for dz in (0, 1) for dy in (0, -1, 1) for dx in (-1, 1)]
NEAR += [(0, dy, dz) for dy, dz in GROUPS[:0:-1]]
POS, FEAT, GRAD, FORCE = 0, 1, 2, 3
GROUP = 2 * 128
TILE = 16
PART = 256
ROWS = 16


def nn(a, b, **kw):
    return jnp.dot(a, b, preferred_element_type=F32, **kw)


def nt(a, b, **kw):
    return lax.dot_general(a, b, (((1,), (1,)), ((), ())), preferred_element_type=F32, **kw)


def tn(a, b, **kw):
    return lax.dot_general(a, b, (((0,), (0,)), ((), ())), preferred_element_type=F32, **kw)


def poly(x, coefficients):
    total = coefficients[-1]
    for c in coefficients[-2::-1]:
        total = total * x + c
    return total


COS_C = [(-1.0) ** i * math.pi ** (2 * i) / math.factorial(2 * i) for i in range(8)]
SIN_C = [(-1.0) ** i * math.pi ** (2 * i + 1) / math.factorial(2 * i + 1) for i in range(7)]


def geometry(vx, vy, vz, w, derivative):
    sq = jnp.where(w > 0.0, vx * vx + vy * vy + vz * vz, 1.0)
    inv_r = lax.rsqrt(sq)
    r = sq * inv_r
    ux, uy, uz = vx * inv_r, vy * inv_r, vz * inv_r
    s = jnp.minimum(r * (1.0 / CUTOFF), 1.0)
    t = 1.0 - s * s
    x = s - 0.5
    x2 = x * x
    sin1 = poly(x2, COS_C)
    cos1 = -x * poly(x2, SIN_C)
    p = w * ((2.0 / CUTOFF) ** 0.5 * inv_r)
    pt = p * t
    q = pt * t
    twice = 2.0 * cos1
    sins = [sin1, twice * sin1]
    for k in range(2, NB):
        sins.append(twice * sins[-1] - sins[-2])
    basis = [q * v for v in sins]
    if not derivative:
        return (ux, uy, uz), inv_r, basis, None
    coss = [cos1, twice * cos1 - 1.0]
    for k in range(2, NB):
        coss.append(twice * coss[-1] - coss[-2])
    q5 = q * (math.pi / CUTOFF)
    low = q * inv_r + pt * (s * (4.0 / CUTOFF))
    slopes = [(k + 1.0) * q5 * coss[k] - low * sins[k] for k in range(NB)]
    return (ux, uy, uz), inv_r, basis, slopes


def harmonics(ux, uy, uz):
    return [
        None,
        R3 * ux,
        R3 * uy,
        R3 * uz,
        R15 * ux * uy,
        R15 * uy * uz,
        0.5 * R5 * (3.0 * uz * uz - 1.0),
        R15 * ux * uz,
        0.5 * R15 * (ux * ux - uy * uy),
    ]


def edge_pull(gamma, unit, inv_r, basis, slopes):
    ux, uy, uz = unit
    ang = harmonics(ux, uy, uz)
    q = [gamma(0, k) for k in range(NB)]

    def radial_sum(m):
        total = None
        for k in range(NB):
            value = gamma(m, k)
            q[k] = q[k] + value * ang[m]
            term = value * basis[k]
            total = term if total is None else total + term
        return total

    gx, gy, gz = (R3 * radial_sum(m) for m in (1, 2, 3))
    p = R15 * radial_sum(4)
    gx, gy = gx + uy * p, gy + ux * p
    p = R15 * radial_sum(5)
    gy, gz = gy + uz * p, gz + uy * p
    gz = gz + (3.0 * R5) * uz * radial_sum(6)
    p = R15 * radial_sum(7)
    gx, gz = gx + uz * p, gz + ux * p
    p = R15 * radial_sum(8)
    gx, gy = gx + ux * p, gy - uy * p
    radial = q[0] * slopes[0]
    for k in range(1, NB):
        radial = radial + q[k] * slopes[k]
    along = radial - (gx * ux + gy * uy + gz * uz) * inv_r
    return gx * inv_r + along * ux, gy * inv_r + along * uy, gz * inv_r + along * uz


def squares(parts):
    total = parts[0] * parts[0]
    for part in parts[1:]:
        total = total + part * part
    return total


def split(x, parts):
    out = []
    for _ in range(parts):
        part = x.astype(BF16)
        out.append(part)
        x = x - part.astype(F32)
    return out


def equal(a, b):
    return jnp.where(a == b, 1.0, 0.0).astype(BF16)


def over(count, step, body):
    if step == count:
        body(0, step)
        return

    def run(i, carry):
        body(i, step)
        return carry

    lax.fori_loop(0, count // step, run, 0)


def flip(offset):
    dx, dy, dz = offset
    return (-dx, -dy, dz)


def kernel(
    *refs,
):
    given, (e_out, f_out) = refs[:15], refs[15:17]
    held, loaded = refs[17:32], refs[32]
    pos, occ, nbr, keep, fx, fy, fz, r1, mix1, emb, r2, mix2, ro1, rht, ro2 = held
    (
        xt, psend, precv, xcol, nbrs, key, local, weight, hot, ohx, ohxt, oh, oht,
        r1b, r2b, mixt1, mixt2, embb, moments, amp, amp2, pulls, inv, ht, hn, hx, hrecv, smat, geo, near, ut, un, dghost,
        gam, dv, dh, gsend, grecv, frow, pulled, fsend, frecv, dm, dvl, flat,
        send, recv,
    ) = refs[33:]
    cx, cy, cz = lax.axis_index("gx"), lax.axis_index("gy"), lax.axis_index("gz")
    nx, ny, nz = lax.axis_size("gx"), lax.axis_size("gy"), lax.axis_size("gz")

    def device(offset):
        dx, dy, dz = offset
        return (lax.rem(cx + dx + nx, nx), lax.rem(cy + dy + ny, ny), lax.rem(cz + dz, nz))

    def copy(phase, offset, src, dst):
        i = NEAR.index(offset)
        j = NEAR.index(flip(offset))
        return pltpu.make_async_remote_copy(
            src_ref=src, dst_ref=dst, send_sem=send.at[phase, i], recv_sem=recv.at[phase, j],
            device_id=device(offset), device_id_type=MESH,
        )

    def exchange(phase, source, target):
        copies = [copy(phase, o, source(o), target(o)) for o in NEAR]
        for c in copies:
            c.start()
        return copies

    def finish(copies):
        for c in copies:
            c.wait_recv()
        for c in copies:
            c.wait_send()

    def rows_of(offset, along):
        dx, dy, dz = offset
        base = GROUPS.index((dy, dz)) * GROUP
        if along == 0:
            return pl.ds(base, ATOMS)
        return pl.ds(base + ATOMS + (0 if along < 0 else ATOMS // 2), ATOMS // 2)

    barrier = pltpu.get_barrier_semaphore()
    for offset in NEAR:
        pl.semaphore_signal(barrier, inc=1, device_id=device(offset), device_id_type=MESH)
    loads = [
        pltpu.make_async_copy(given[n], held[n], loaded.at[n]) for n in range(len(held))
    ]
    order = [0, 4, 5, 6, 2, 3, 7, 10, 8, 11, 9, 12, 1, 13, 14]
    for n in order:
        loads[n].start()
    for n in order[:4]:
        loads[n].wait()

    row = lax.broadcasted_iota(jnp.int32, (8, ATOMS), 0)
    lane = lax.broadcasted_iota(jnp.int32, (8, ATOMS), 1)

    def pick(ids, tiles):
        low = ids & (ATOMS - 1)
        total = jnp.take_along_axis(tiles[0], low, axis=1)
        for b in range(1, len(tiles)):
            here = jnp.take_along_axis(tiles[b], low, axis=1)
            total = jnp.where(ids >= b * ATOMS, here, total)
        return total

    psend[...] = jnp.zeros((2, 8, ATOMS), F32)
    for d in range(3):
        psend[0, d : d + 1, :] = pos[d, 0, 0]
    psend[0, 3:4, :] = fy[0, 0, 0, 1:2, :].astype(F32)
    psend[0, 4:5, :] = fy[0, 0, 0, 0:1, :].astype(F32)
    psend[0, 5:6, :] = fz[0, 0].astype(F32)
    xt[0] = psend[0]
    pick_x = jnp.concatenate([fx[0, 0, 0, 1:2, :], fx[0, 0, 0, 0:1, :]], axis=1)
    psend[1] = pick(jnp.broadcast_to(pick_x, (8, ATOMS)), [xt[0]])
    for n in order[4:6]:
        loads[n].wait()
    def list_row(j, carry):
        slot = nbr[j, 0, 0]
        nbrs[pl.ds(j, 1), :] = slot
        value = jnp.where(keep[j, 0, 0] > 0, slot, -1)
        key[pl.ds(j, 1), :] = value
        for b in range(5):
            inside = (value >= b * ATOMS) & (value < (b + 1) * ATOMS)
            inside = jnp.where(inside, value - b * ATOMS, -1).astype(F32)
            local[b, j] = jnp.broadcast_to(inside, (16, ATOMS)).astype(BF16)
        return carry

    lax.fori_loop(0, NEIGH, list_row, 0, unroll=2)
    for n in order[6:]:
        loads[n].wait()
    def spread_row(k, carry):
        r1b[k] = SPREAD * jnp.broadcast_to(r1[pl.ds(k, 1), :], (C, ATOMS)).T
        r2b[k] = SPREAD * jnp.broadcast_to(r2[pl.ds(k, 1), :], (C, ATOMS)).T
        return carry

    lax.fori_loop(0, NB, spread_row, 0)
    for b in range(3):
        rows = slice(b * C, (b + 1) * C)
        mixt1[:, rows] = mix1[rows, :].astype(F32).T.astype(BF16)
        mixt2[:, rows] = mix2[rows, :].astype(F32).T.astype(BF16)
    embb[0] = jnp.broadcast_to(emb[...], (C, ATOMS)).T
    embb[1] = jnp.broadcast_to(ro1[...], (C, ATOMS)).T
    pl.semaphore_wait(barrier, len(NEAR))
    copies = exchange(
        POS,
        lambda o: psend.at[1 if o[0] else 0],
        lambda o: precv.at[NEAR.index(flip(o))],
    )

    row16 = lax.broadcasted_iota(jnp.int32, (16, ATOMS), 0).astype(F32)
    one16 = jnp.ones((16, ATOMS), BF16)
    nil16 = jnp.zeros((16, ATOMS), BF16)

    def weight_block(n, carry):
        b = n // 4
        i = n % 4
        ids = [(row16 + (i * 32 + 16 * t).astype(F32)).astype(BF16) for t in range(2)]
        at = [pl.ds(pl.multiple_of(n * 32 + 16 * t, 16), 16) for t in range(2)]

        def scan(j8, total):
            total = list(total)
            for jj in range(8):
                one = local[b, j8 * 8 + jj]
                to = pl.ds(pl.multiple_of((j8 * 8 + jj) * ATOMS, ATOMS), ATOMS)
                for t in range(2):
                    found = jnp.where(ids[t] == one, one16, nil16)
                    hot[at[t], to] = found
                    total[t] = total[t] + found
            return tuple(total)

        total = lax.fori_loop(0, NEIGH // 8, scan, (nil16, nil16))
        for t in range(2):
            weight[at[t], :] = total[t].astype(F32)
        return carry

    lax.fori_loop(0, EXT // 32, weight_block, 0)
    square = (ATOMS, ATOMS)
    sub = lax.broadcasted_iota(jnp.int32, square, 0)
    along = lax.broadcasted_iota(jnp.int32, square, 1)
    ohx[...] = equal(sub, jnp.broadcast_to(pick_x, square))
    ohxt[...] = equal(along.astype(F32), jnp.broadcast_to(pick_x, square).astype(F32).T)
    finish(copies)

    def received(dx, dy, dz):
        return precv[NEAR.index((dx, dy, dz))]

    def column(dy, dz):
        own = xt[0] if (dy, dz) == (0, 0) else received(0, dy, dz)
        side = jnp.where(lane < ATOMS // 2, received(-1, dy, dz), received(1, dy, dz))
        step = jnp.where(lane < ATOMS // 2, -STEP_XY, STEP_XY)
        side = side + jnp.where(row == 0, step, 0.0)
        shift = jnp.where(row == 1, dy * STEP_XY, 0.0)
        return [own, side] if dy == 0 else [own + shift, side + shift]

    def listed(dy, dz):
        source = received(0, dy, dz)
        at = 3 if dy < 0 else 4
        return jnp.broadcast_to(source[at : at + 1, :], (8, ATOMS)).astype(jnp.int32)

    own, side = column(0, 0)
    xt[1] = side
    low_y, high_y = listed(-1, 0), listed(1, 0)
    xt[2] = pick(low_y, column(-1, 0))
    xt[3] = pick(high_y, column(1, 0))
    other = jnp.broadcast_to(received(0, 0, 1)[5:6, :], (8, ATOMS)).astype(jnp.int32)
    low_bits = other & (ATOMS - 1)
    through_low = jnp.take_along_axis(listed(-1, 1), low_bits, axis=1)
    through_high = jnp.take_along_axis(listed(1, 1), low_bits, axis=1)
    far = jnp.where(other < 2 * ATOMS, other, through_low + 2 * ATOMS)
    far = jnp.where(other < 3 * ATOMS, far, through_high + 4 * ATOMS)
    upward = jnp.where(cz == 0, STEP_Z, -STEP_Z)
    xt[4] = pick(far, column(0, 1) + column(-1, 1) + column(1, 1)) + jnp.where(row == 2, upward, 0.0)

    moments[...] = jnp.zeros(moments.shape, F32)

    def list_tile(i, carry):
        at = pl.ds(pl.multiple_of(i * 8, 8), 8)
        ids = nbrs[at, :]
        kept = jnp.where(key[at, :] >= 0, 1.0, 0.0)
        offset = []
        for d in range(3):
            tables = [jnp.broadcast_to(xt[b, d : d + 1, :], (8, ATOMS)) for b in range(5)]
            offset.append(pick(ids, tables) - tables[0])
        unit, inv_r, basis, slopes = geometry(*offset, kept, True)
        for k in range(NB):
            near[k, at, :] = basis[k]
            near[NB + k, at, :] = slopes[k]
        for d in range(3):
            near[2 * NB + d, at, :] = unit[d]
        near[2 * NB + 3, at, :] = inv_r
        ang = harmonics(*unit)
        for m in range(NM):
            for k in range(NB):
                moments[m * NB + k] += basis[k] if m == 0 else basis[k] * ang[m]
        return carry

    lax.fori_loop(0, NEIGH // 8, list_tile, 0)

    def first_amplitude(i, step):
        for m in range(step):
            m = i * step + m
            total = None
            for k in range(NB):
                term = r1b[k] * jnp.sum(moments[m * NB + k], axis=0, keepdims=True)
                total = term if k == 0 else total + term
            amp[m] = total

    over(NM, 3, first_amplitude)
    inv[0:C, :] = amp[0].astype(BF16)
    inv[C : 2 * C, :] = squares([amp[m] for m in range(1, 4)]).astype(BF16)
    inv[2 * C :, :] = squares([amp[m] for m in range(4, 9)]).astype(BF16)
    ht[0] = (nn(mixt1[...], inv[...]) + embb[0]).astype(BF16)
    hrecv[0:ATOMS, :] = ht[0].T
    hx[...] = nn(ohxt[...], hrecv[0:ATOMS, :]).astype(BF16)
    half = ATOMS // 2

    def feature_source(o):
        if o[0] == 0:
            return hrecv.at[pl.ds(0, ATOMS), :]
        return hx.at[pl.ds(0 if o[0] > 0 else half, half), :]

    copies = exchange(FEAT, feature_source, lambda o: hrecv.at[rows_of(flip(o), -o[0]), :])

    for b in range(5):
        xcol[b * ATOMS : (b + 1) * ATOMS, :] = xt[b].T
    column_ids = [
        jnp.broadcast_to(ids[0:1, :], square).astype(F32).T for ids in (low_y, high_y, far)
    ]
    row_ids = [jnp.broadcast_to(ids[0:1, :], square) for ids in (low_y, high_y, far)]
    at = 0
    for ids, ids_t, blocks in zip(row_ids, column_ids, (2, 2, 6)):
        for b in range(blocks):
            cut = slice(at * ATOMS, (at + 1) * ATOMS)
            oht[cut, :] = equal(sub + b * ATOMS, ids)
            oh[:, cut] = equal((along + b * ATOMS).astype(F32), ids_t)
            at = at + 1

    def planes(i, carry):
        at = pl.ds(pl.multiple_of(i * ROWS, ROWS), ROWS)
        columns = xcol[at, :]
        v = [columns[:, d : d + 1] - xt[0, d : d + 1, :] for d in range(3)]
        unit, inv_r, basis, slopes = geometry(*v, weight[at, :], True)
        for k in range(NB):
            geo[k, at, :] = basis[k]
            geo[NB + k, at, :] = slopes[k]
        for d in range(3):
            geo[2 * NB + d, at, :] = unit[d]
        geo[2 * NB + 3, at, :] = inv_r
        ang = harmonics(*unit)
        for m in range(NM):
            for k in range(NB):
                product = basis[k] if m == 0 else basis[k] * ang[m]
                col = (m * NB + k) * ATOMS
                smat[at, col : col + ATOMS] = product.astype(BF16)
        return carry

    lax.fori_loop(0, EXT // ROWS, planes, 0, unroll=2)
    def chunk(m, step=1):
        width = NB * ATOMS * step
        if isinstance(m, int):
            return pl.ds(m * width, width)
        return pl.ds(pl.multiple_of(m * width, width), width)

    def amplitude(m, source, rows):
        part = nn(source, smat[rows, chunk(m)])
        total = None
        for k in range(NB):
            term = r2b[k] * part[:, k * ATOMS : (k + 1) * ATOMS]
            total = term if k == 0 else total + term
        return total

    def amplitude_own(i, step):
        for t in range(step):
            amp2[i * step + t] = amplitude(i * step + t, ht[0], slice(0, ATOMS))

    over(NM, 9, amplitude_own)
    finish(copies)
    hn[0:GROUP, :] = hrecv[0:GROUP, :]
    for b, first, blocks in ((2, 0, 2), (3, 2, 2), (4, 4, 6)):
        cut = slice(first * ATOMS, (first + blocks) * ATOMS)
        source = hrecv[GROUP + first * ATOMS : GROUP + (first + blocks) * ATOMS, :]
        hn[b * ATOMS : (b + 1) * ATOMS, :] = nn(oh[:, cut], source).astype(BF16)
    for b in range(1, 5):
        ht[b] = hn[b * ATOMS : (b + 1) * ATOMS, :].T

    whole = jnp.concatenate([ht[b] for b in range(1, 5)], axis=1)
    def amplitude_ghosts(i, step):
        for t in range(step):
            amp2[i * step + t] += amplitude(i * step + t, whole, slice(ATOMS, EXT))

    over(NM, 9, amplitude_ghosts)
    inv[0:C, :] = amp2[0].astype(BF16)
    inv[C : 2 * C, :] = squares([amp2[m] for m in range(1, 4)]).astype(BF16)
    inv[2 * C :, :] = squares([amp2[m] for m in range(4, 9)]).astype(BF16)
    own = ht[0].astype(F32)
    h2 = nn(mixt2[...], inv[...]) + own
    pre = nn(rht[...], h2, precision=HIGHEST)
    sig = 1.0 / (1.0 + jnp.exp(-pre))
    filled = occ[0, 0].astype(F32)
    energy = nn(ro1[...], own, precision=HIGHEST) + nn(ro2[...], pre * sig, precision=HIGHEST)
    e_out[0, 0] = filled * energy
    dpre = tn(ro2[...], filled, precision=HIGHEST) * (sig * (1.0 + pre * (1.0 - sig)))
    dh2 = tn(rht[...], dpre, precision=HIGHEST)
    dinv = nn(mix2[...], dh2.astype(BF16))
    pulls[...] = dinv

    def pulled_amplitude(m, values):
        square = jnp.where(m < 4, pulls[C : 2 * C, :], pulls[2 * C :, :])
        return jnp.where(m == 0, pulls[0:C, :], 2.0 * square * values[m])

    def rows_two(i, step):
        for t in range(step):
            m = i * step + t
            g = pulled_amplitude(m, amp2)
            turned = SPREAD * g.T
            for k in range(NB):
                at = pl.ds(pl.multiple_of((m * NB + k) * ATOMS, ATOMS), ATOMS)
                ut[:, at] = (r2b[k] * g).astype(BF16)
                un[at, :] = (turned * r2[k : k + 1, :]).astype(BF16)

    over(NM, 9, rows_two)

    def ghost_part(i, step):
        part = nn(smat[ATOMS:, chunk(i, step)], un[chunk(i, step), :])
        if step == NM:
            dghost[...] = part
        else:
            dghost[...] += part

    if 9 < NM:
        dghost[...] = jnp.zeros(dghost.shape, F32)
    over(NM, 9, ghost_part)
    ghosts = dghost[...].astype(BF16)
    gsend[ATOMS:GROUP, :] = ghosts[0:ATOMS, :]
    for b, first, blocks in ((1, 0, 2), (2, 2, 2), (3, 4, 6)):
        cut = slice(first * ATOMS, (first + blocks) * ATOMS)
        rows = slice(GROUP + first * ATOMS, GROUP + (first + blocks) * ATOMS)
        gsend[rows, :] = nn(oht[cut, :], ghosts[b * ATOMS : (b + 1) * ATOMS, :]).astype(BF16)
    copies = exchange(
        GRAD,
        lambda o: gsend.at[rows_of(o, o[0]), :],
        lambda o: grecv.at[rows_of(flip(o), o[0]), :],
    )
    dh[...] = (dh2 + embb[1] * filled).T

    def own_part(i, step):
        dh[...] += nn(smat[0:ATOMS, chunk(i, step)], un[chunk(i, step), :])

    over(NM, 3, own_part)

    def load(planes, at):
        return (
            [planes[2 * NB + d, at, :] for d in range(3)],
            planes[2 * NB + 3, at, :],
            [planes[k, at, :] for k in range(NB)],
            [planes[NB + k, at, :] for k in range(NB)],
        )

    zero = jnp.zeros((TILE, ATOMS), F32)
    totals = (zero, zero, zero)

    def pull_part(base, count, step, totals):
        def gammas(i, step):
            for t in range(step):
                at = chunk(i * step + t)
                gam[0:count, at] = nn(hn[pl.ds(base, count), :], ut[:, at])

        over(NM, step, gammas)

        def pull_two(i, totals):
            here = pl.ds(pl.multiple_of(i * TILE, TILE), TILE)
            at = pl.ds(pl.multiple_of(base + i * TILE, TILE), TILE)

            def gamma(m, k):
                col = (m * NB + k) * ATOMS
                return gam[here, col : col + ATOMS]

            out = edge_pull(gamma, *load(geo, at))
            for d in range(3):
                dv[d, at, :] = out[d]
            return tuple(totals[d] + out[d] for d in range(3))

        return lax.fori_loop(0, count // TILE, pull_two, totals)

    def ghost_pull(b, totals):
        return pull_part(pl.multiple_of(ATOMS + b * PART, ATOMS), PART, NM, totals)

    totals = lax.fori_loop(0, 4 * ATOMS // PART, ghost_pull, totals)

    def lines_two(first, last):
        rows = slice(first, last)
        total = None
        for d in range(3):
            take = jnp.where(along == 2 * d, 1.0, 0.0).astype(BF16)
            for part in split(dv[d, rows, :], 2):
                term = nn(part, take)
                total = term if total is None else total + term
        for b in range((last - first) // ATOMS):
            lines = total[b * ATOMS : (b + 1) * ATOMS, :].T
            for d in range(3):
                at = slice(first + b * ATOMS, first + (b + 1) * ATOMS)
                frow[d : d + 1, at] = lines[2 * d : 2 * d + 1, :]

    lines_two(ATOMS, EXT)
    finish(copies)
    slot_sum = dh[...]
    for g in range(1, 6):
        slot_sum = slot_sum + grecv[g * GROUP : g * GROUP + ATOMS, :].astype(F32)
    pick_sum = grecv[ATOMS:GROUP, :].astype(F32)
    for g in range(1, 6):
        pick_sum = pick_sum + grecv[g * GROUP + ATOMS : (g + 1) * GROUP, :].astype(F32)
    hi, low = split(pick_sum, 2)
    dh1 = slot_sum + nn(ohx[...], hi) + nn(ohx[...], low)

    dinv = nt(mix1[...], dh1.astype(BF16))
    pulls[...] = dinv

    def rows_one(i, step):
        for t in range(step):
            m = i * step + t
            lines = SPREAD * nn(r1[...], pulled_amplitude(m, amp), precision=HIGHEST)
            for k in range(NB):
                dm[m * NB + k] = jnp.broadcast_to(lines[k : k + 1, :], (8, ATOMS))

    over(NM, 3, rows_one)

    def pull_one(i, carry):
        at = pl.ds(pl.multiple_of(i * 8, 8), 8)
        out = edge_pull(lambda m, k: dm[m * NB + k], *load(near, at))
        for d in range(3):
            for part, value in enumerate(split(out[d], 2)):
                dvl[2 * d + part, at, :] = value.astype(F32)
        return carry

    lax.fori_loop(0, NEIGH // 8, pull_one, 0, unroll=7)
    flat[6:8, :] = jnp.zeros((2, NEIGH * ATOMS), F32)

    def flat_row(j, carry):
        to = pl.ds(pl.multiple_of(j * ATOMS, ATOMS), ATOMS)
        for n in range(6):
            flat[n : n + 1, to] = dvl[n, pl.ds(j, 1), :]
        return carry

    lax.fori_loop(0, NEIGH, flat_row, 0, unroll=4)

    packed = flat[...].astype(BF16)

    def lines_of(first, last):
        wide = nt(packed, hot[first:last, :])
        for d in range(3):
            frow[d : d + 1, first:last] += wide[2 * d : 2 * d + 1, :] + wide[2 * d + 1 : 2 * d + 2, :]

    lines_of(ATOMS, EXT)

    def thrice(values):
        pad = jnp.zeros((1, values.shape[1]), F32)
        parts = [jnp.concatenate([p.astype(F32), pad], axis=0) for p in split(values, 3)]
        return jnp.concatenate(parts + [jnp.zeros((4, values.shape[1]), F32)], axis=0).astype(BF16)

    def merged(wide):
        return wide[0:3, :] + wide[4:7, :] + wide[8:11, :]

    fsend[...] = jnp.zeros(fsend.shape, F32)
    fsend[0, 0:3, :] = frow[0:3, ATOMS:GROUP]
    at = 0
    for b, blocks in ((2, 2), (3, 2), (4, 6)):
        cut = slice(at * ATOMS, (at + blocks) * ATOMS)
        values = merged(nn(thrice(frow[0:3, b * ATOMS : (b + 1) * ATOMS]), oh[:, cut]))
        for n in range(blocks):
            fsend[1 + at + n, 0:3, :] = values[:, n * ATOMS : (n + 1) * ATOMS]
        at = at + blocks

    def force_source(o):
        g = GROUPS.index((o[1], o[2]))
        return fsend.at[2 * g - 1 + (1 if o[0] else 0)]

    copies = exchange(FORCE, force_source, lambda o: frecv.at[NEAR.index(flip(o))])
    totals = pull_part(0, ATOMS, 3, totals)
    lines_two(0, ATOMS)
    for d in range(3):
        pulled[d : d + 1, :] = jnp.sum(totals[d], axis=0, keepdims=True)
    lines_of(0, ATOMS)
    for d in range(3):
        pulled[d : d + 1, :] += jnp.sum(dvl[2 * d] + dvl[2 * d + 1], axis=0, keepdims=True)
    finish(copies)
    slot_sum = frow[0:3, 0:ATOMS] - pulled[0:3, :]
    from_low = from_high = None
    for dy, dz in GROUPS:
        if (dy, dz) != (0, 0):
            slot_sum = slot_sum + frecv[NEAR.index((0, dy, dz)), 0:3, :]
        up, down = (frecv[NEAR.index((dx, dy, dz)), 0:3, :] for dx in (1, -1))
        from_high = up if from_high is None else from_high + up
        from_low = down if from_low is None else from_low + down
    pick_sum = jnp.where(lane[0:3, :] < half, from_high, from_low)
    total = slot_sum + merged(nt(thrice(pick_sum), ohx[...]))
    for d in range(3):
        f_out[d, 0, 0] = -total[d : d + 1, :]


def per_device(
    positions, occupancy, neighbours, keep, face_x, face_y, face_z, radial_one, mix_one, embed,
    radial_two, mix_two, read_one, read_hidden, read_out,
):
    vmem = pl.BlockSpec(memory_space=pltpu.VMEM)
    cols = NB * NM * ATOMS
    operands = (
        positions, occupancy, neighbours, keep, face_x, face_y, face_z, radial_one, mix_one,
        embed.reshape(1, -1), radial_two, mix_two, read_one.reshape(1, -1), read_hidden.T,
        read_out.reshape(1, -1),
    )
    scratch = [pltpu.VMEM(v.shape, v.dtype) for v in operands]
    scratch += [
        pltpu.SemaphoreType.DMA((len(operands),)),
        pltpu.VMEM((5, 8, ATOMS), F32),
        pltpu.VMEM((2, 8, ATOMS), F32),
        pltpu.VMEM((17, 8, ATOMS), F32),
        pltpu.VMEM((EXT, 8), F32),
        pltpu.VMEM((NEIGH, ATOMS), jnp.int32),
        pltpu.VMEM((NEIGH, ATOMS), jnp.int32),
        pltpu.VMEM((5, NEIGH, 16, ATOMS), BF16),
        pltpu.VMEM((EXT, ATOMS), F32),
        pltpu.VMEM((EXT, NEIGH * ATOMS), BF16),
        pltpu.VMEM((ATOMS, ATOMS), BF16),
        pltpu.VMEM((ATOMS, ATOMS), BF16),
        pltpu.VMEM((ATOMS, 10 * ATOMS), BF16),
        pltpu.VMEM((10 * ATOMS, ATOMS), BF16),
        pltpu.VMEM((NB, C, ATOMS), F32),
        pltpu.VMEM((NB, C, ATOMS), F32),
        pltpu.VMEM((C, 3 * C), BF16),
        pltpu.VMEM((C, 3 * C), BF16),
        pltpu.VMEM((2, C, ATOMS), F32),
        pltpu.VMEM((NB * NM, 8, ATOMS), F32),
        pltpu.VMEM((NM, C, ATOMS), F32),
        pltpu.VMEM((NM, C, ATOMS), F32),
        pltpu.VMEM((3 * C, ATOMS), F32),
        pltpu.VMEM((3 * C, ATOMS), BF16),
        pltpu.VMEM((5, C, ATOMS), BF16),
        pltpu.VMEM((EXT, C), BF16),
        pltpu.VMEM((ATOMS, C), BF16),
        pltpu.VMEM((6 * GROUP, C), BF16),
        pltpu.VMEM((EXT, cols), BF16),
        pltpu.VMEM((2 * NB + 4, EXT, ATOMS), F32),
        pltpu.VMEM((2 * NB + 4, NEIGH, ATOMS), F32),
        pltpu.VMEM((C, cols), BF16),
        pltpu.VMEM((cols, C), BF16),
        pltpu.VMEM((4 * ATOMS, C), F32),
        pltpu.VMEM((PART, cols), F32),
        pltpu.VMEM((3, EXT, ATOMS), F32),
        pltpu.VMEM((ATOMS, C), F32),
        pltpu.VMEM((6 * GROUP, C), BF16),
        pltpu.VMEM((6 * GROUP, C), BF16),
        pltpu.VMEM((8, EXT), F32),
        pltpu.VMEM((8, ATOMS), F32),
        pltpu.VMEM((11, 8, ATOMS), F32),
        pltpu.VMEM((17, 8, ATOMS), F32),
        pltpu.VMEM((NB * NM, 8, ATOMS), F32),
        pltpu.VMEM((6, NEIGH, ATOMS), F32),
        pltpu.VMEM((8, NEIGH * ATOMS), F32),
        pltpu.SemaphoreType.DMA((4, 17)),
        pltpu.SemaphoreType.DMA((4, 17)),
    ]
    return pl.pallas_call(
        kernel,
        out_shape=(
            jax.ShapeDtypeStruct(occupancy.shape, F32),
            jax.ShapeDtypeStruct(positions.shape, F32),
        ),
        in_specs=[pl.BlockSpec(memory_space=pl.ANY)] * len(operands),
        out_specs=(vmem, vmem),
        scratch_shapes=scratch,
        compiler_params=pltpu.CompilerParams(
            collective_id=0, has_side_effects=True, vmem_limit_bytes=56 * 1024 * 1024
        ),
    )(*operands)


def solution(mesh):
    return jax.shard_map(
        per_device,
        mesh=mesh,
        in_specs=(
            P(None, "gx", "gy", "gz", None),
            P("gx", "gy", "gz", None),
            P(None, "gx", "gy", "gz", None),
            P(None, "gx", "gy", "gz", None),
            P("gx", "gy", "gz", None, None),
            P("gx", "gy", "gz", None, None),
            P("gx", "gy", "gz", None),
            P(),
            P(),
            P(),
            P(),
            P(),
            P(),
            P(),
            P(),
        ),
        out_specs=(P("gx", "gy", "gz", None), P(None, "gx", "gy", "gz", None)),
        check_vma=False,
    )
```
